128 devices in a mesh: row: 16 (over x, y), col: 8 (over z, core).
Axes of the slice: x: 4, y: 4, z: 4, core: 2. Of those that a mesh axis runs over, the one named last changes fastest.
Arguments:
- inputs: bfloat16 [512, 12288], P('col', 'row'), may hold values from -6 to 6
- w_up: bfloat16 [12288, 24576], P('row', 'col'), may hold values from -0.0546875 to 0.0546875
- w_down: bfloat16 [24576, 12288], P('col', 'row'), may hold values from -0.0390625 to 0.0390625
- mask_up: int32 [96, 192], P('row', 'col'), may hold values from 0 to 1, as said below
- mask_down: int32 [192, 96], P('col', 'row'), may hold values from 0 to 1, as said below
- cotangent: bfloat16 [512, 12288], P('col', 'row'), may hold values from -1.5 to 1.5
Outputs:
- outputs: bfloat16 [512, 12288], P('col', 'row')
- grad_inputs: bfloat16 [512, 12288], P('col', 'row')
- grad_up: bfloat16 [12288, 24576], P('row', 'col')
- grad_down: bfloat16 [24576, 12288], P('col', 'row')
The draws below stay inside these ranges and needn't reach their ends.
Inputs may be any that keep to these rules, and one draw needn't show every extreme that they name: `mask_up`: each entry is 0 or 1; the chance of a 1 is the same along a row of tiles and differs from row to row, between 0.2 and 0.8. `mask_down`: each entry is 0 or 1; the chance of a 1 is the same along a row of tiles and differs from row to row, between 0.2 and 0.8.
All inputs are finite; a program needn't handle non-finite values.
Results may differ from the reference program's by a relative error of at most 0.029.
Values may be sent and summed in bfloat16 or wider, within the bound.
A program may use at most 128 MiB of HBM per device.

```python
import jax
import jax.numpy as jnp

D = 12288
FF = 24576
TILE = 128
TOKENS = 512
N_ROW = 16
N_COL = 8


def tile_pattern(key, rows, cols):
    key_level, key_tick = jax.random.split(key)
    levels = jax.random.randint(key_level, (rows, 1), 20, 81)
    ticks = jax.random.randint(key_tick, (rows, cols), 0, 100)
    return (ticks < levels).astype(jnp.int32)


def draw_mask_up(key, part):
    key = jax.random.fold_in(key, 11)
    return tile_pattern(key, D // TILE, FF // TILE)


def draw_mask_down(key, part):
    key = jax.random.fold_in(key, 23)
    return tile_pattern(key, FF // TILE, D // TILE)


def steps_of(own_key, shape, shards, least, largest):
    def one(axis_at, shards_of):
        heights = jax.random.uniform(jax.random.fold_in(jax.random.fold_in(own_key, 6), axis_at), (shards_of,), jnp.float32, least / len(shards), largest / len(shards))
        return jnp.repeat(jnp.exp(heights), shape[axis_at] // shards_of).reshape((-1,) + (1,) * (len(shape) - axis_at - 1))

    gain = one(*shards[0])
    for cut in shards[1:]:
        gain = gain * one(*cut)
    return gain


def normal_values(key, dims, deviation, limit, shards=(), held_as=jnp.bfloat16):
    level = steps_of(key, dims, shards, -0.22, 0.18) if shards else 1.0
    drawn = jax.random.normal(key, dims, jnp.float32) * deviation * level
    return jnp.minimum(jnp.maximum(drawn, -limit), limit).astype(held_as)


def setup_inputs(seed: int = 0) -> dict:
    key_of = jax.random.split(jax.random.key(seed), 7)
    inputs = normal_values(key_of[0], (TOKENS, D), 1.0, 6.0, ((0, 8), (1, 16)))
    w_up = normal_values(key_of[1], (D, FF), D ** -0.5, 0.0546875, ((0, 16), (1, 8)))
    w_down = normal_values(key_of[2], (FF, D), FF ** -0.5, 0.0390625, ((0, 8), (1, 16)))
    mask_up = draw_mask_up(jax.random.fold_in(key_of[6], 71), 0)
    mask_down = draw_mask_down(jax.random.fold_in(key_of[6], 71), 0)
    cotangent = normal_values(key_of[5], (TOKENS, D), 0.25, 1.5, ((0, 8), (1, 16)))
    return dict(inputs=inputs, w_up=w_up, w_down=w_down, mask_up=mask_up, mask_down=mask_down, cotangent=cotangent)


def apply_mask(weight, mask):
    rows, cols = mask.shape
    tile = weight.shape[0] // rows
    shaped = weight.reshape(rows, tile, cols, tile)
    keep = mask[:, None, :, None].astype(weight.dtype)
    return (shaped * keep).reshape(weight.shape)

def smooth_gate(value):
    return jax.nn.gelu(value, approximate=True)

def reference(inputs, w_up, w_down, mask_up, mask_down, cotangent):
    up_kept = apply_mask(w_up, mask_up)
    down_kept = apply_mask(w_down, mask_down)
    feat = D // N_ROW
    hunits = FF // N_COL
    hidden = jnp.zeros((TOKENS, FF), jnp.float32)
    grad_act = jnp.zeros((TOKENS, FF), jnp.float32)
    for block in range(N_ROW):
        lo = block * feat
        part = jnp.dot(inputs[:, lo:lo + feat], up_kept[lo:lo + feat, :], preferred_element_type=jnp.float32)
        hidden = hidden + part.astype(jnp.bfloat16).astype(jnp.float32)
        back = jnp.dot(cotangent[:, lo:lo + feat], down_kept[:, lo:lo + feat].T, preferred_element_type=jnp.float32)
        grad_act = grad_act + back.astype(jnp.bfloat16).astype(jnp.float32)
    act = smooth_gate(hidden).astype(jnp.bfloat16)
    _, pull = jax.vjp(smooth_gate, hidden)
    grad_hidden = pull(grad_act)[0].astype(jnp.bfloat16)
    outputs = jnp.zeros((TOKENS, D), jnp.float32)
    grad_inputs = jnp.zeros((TOKENS, D), jnp.float32)
    grad_up_cols = []
    grad_down_rows = []
    for block in range(N_COL):
        lo = block * hunits
        act_block = act[:, lo:lo + hunits]
        grad_block = grad_hidden[:, lo:lo + hunits]
        part = jnp.dot(act_block, down_kept[lo:lo + hunits, :], preferred_element_type=jnp.float32)
        outputs = outputs + part.astype(jnp.bfloat16).astype(jnp.float32)
        back = jnp.dot(grad_block, up_kept[:, lo:lo + hunits].T, preferred_element_type=jnp.float32)
        grad_inputs = grad_inputs + back.astype(jnp.bfloat16).astype(jnp.float32)
        grad_up_cols.append(jnp.dot(inputs.T, grad_block, preferred_element_type=jnp.float32).astype(jnp.bfloat16))
        grad_down_rows.append(jnp.dot(act_block.T, cotangent, preferred_element_type=jnp.float32).astype(jnp.bfloat16))
    grad_up = apply_mask(jnp.concatenate(grad_up_cols, axis=1), mask_up)
    grad_down = apply_mask(jnp.concatenate(grad_down_rows, axis=0), mask_down)
    return (outputs.astype(jnp.bfloat16), grad_inputs.astype(jnp.bfloat16), grad_up, grad_down)
```

```python
import functools

import jax
import jax.numpy as jnp
from jax import lax
from jax.experimental import pallas as pl
from jax.experimental.pallas import tpu as pltpu
from jax.sharding import PartitionSpec as P

MESH = pl.DeviceIdType.MESH
BF16 = jnp.bfloat16
F32 = jnp.float32
SIDE = 4
CHUNKS = 4
COLS = 8
ROWS = 16
TOK = COLS * ROWS
BLK = TOK // SIDE
FEAT = 768
QW = 768
TILE = 128
SUB = FEAT // TILE
S0, S1, S2, S3, S4, S5, S6, S7, SEMS = 0, 7, 11, 15, 21, 27, 31, 35, 42

ORDER = (
    (0, 0), (0, 1), (1, 0), (0, 2), (1, 1), (0, 3), (2, 0), (1, 2), (2, 1), (1, 3), (3, 0), (2, 2), (3, 1), (2, 3),
    (4, 0), (3, 2), (4, 1), (3, 3), (5, 0), (4, 2), (5, 1), (4, 3), (6, 0), (5, 2), (6, 1), (5, 3), (6, 2), (6, 3),
    (7, 0), (7, 1), (7, 2), (7, 3),
)


def dot(left, right, right_dim):
    return lax.dot_general(left, right, (((1,), (right_dim,)), ((), ())), preferred_element_type=F32)


def block_kernel(
    inputs, w_up, w_down, mask_up, mask_down, cotangent,
    outputs, grad_inputs, x_out, act_out, grad_out,
    xin, up, down, ph, pg, r1h, r1g, r2h, r2g, sh, sg, r3h, r3g, act, grad, po, r7,
    send, recv, wsem, lsem,
):
    row, col = lax.axis_index("row"), lax.axis_index("col")
    x, y = row // SIDE, lax.rem(row, SIDE)

    def turn(v, by):
        return lax.rem(v + by, SIDE)

    def at_x(by):
        return (turn(x, by) * SIDE + y, col)

    def at_y(by):
        return (x * SIDE + turn(y, by), col)

    def col_of(by):
        return lax.rem(col + by, COLS)

    barrier = pltpu.get_barrier_semaphore()
    partners = [at_x(j) for j in (1, 2, 3)] + [at_y(j) for j in (1, 2, 3)] + [(row, col_of(j)) for j in range(1, COLS)]
    for device in partners:
        pl.semaphore_signal(barrier, inc=1, device_id=device, device_id_type=MESH)

    own = [
        pltpu.make_async_copy(inputs, xin.at[:, col, 0], lsem.at[0]),
        pltpu.make_async_copy(cotangent, xin.at[:, col, 1], lsem.at[1]),
    ]
    for copy in own:
        copy.start()
    loads = []
    for q in range(SIDE):
        loads.append(
            (
                pltpu.make_async_copy(w_up.at[:, pl.ds(q * QW, QW)], up.at[q], wsem.at[0, q]),
                pltpu.make_async_copy(w_down.at[pl.ds(q * QW, QW)], down.at[q], wsem.at[1, q]),
            )
        )
    for pair in loads:
        for copy in pair:
            copy.start()
    for copy in own:
        copy.wait()
    pl.semaphore_wait(barrier, len(partners))

    copies = {}

    def ship(c, slot, src, dst, device):
        copy = pltpu.make_async_remote_copy(
            src_ref=src,
            dst_ref=dst,
            send_sem=send.at[c, slot],
            recv_sem=recv.at[c, slot],
            device_id=device,
            device_id_type=MESH,
        )
        copy.start()
        copies[c, slot] = copy

    def land(c, first, last):
        for slot in range(first, last):
            copies[c, slot].wait_recv()

    for c in range(CHUNKS):
        for j in range(1, COLS):
            ship(c, S0 + j - 1, xin.at[c, col], xin.at[c, col], (row, col_of(j)))

    def drop_tiles(q, _):
        def one_row(i, _):
            rows = pl.ds(pl.multiple_of(i * TILE, TILE), TILE)
            for j in range(SUB):
                cols = pl.ds(j * TILE, TILE)
                up[q, rows, cols] = up[q, rows, cols] * mask_up[i, q * SUB + j].astype(F32).astype(BF16)
                down[q, rows, cols] = down[q, rows, cols] * mask_down[q * SUB + i, j].astype(F32).astype(BF16)
            return 0

        return lax.fori_loop(0, SUB, one_row, 0)

    for q in range(SIDE):
        for copy in loads[q]:
            copy.wait()
        drop_tiles(q, 0)

    def multiply_in(c):
        land(c, S0, S1)

        def part(q, _):
            ins = xin[c, :, 0].reshape(TOK, FEAT)
            ph[c, :, q] = dot(ins, up[q], 0).astype(BF16).reshape(SIDE, BLK, QW)
            cot = xin[c, :, 1].reshape(TOK, FEAT)
            pg[c, q] = dot(cot, down[q], 1).astype(BF16).reshape(SIDE, BLK, QW)
            return 0

        lax.fori_loop(0, SIDE, part, 0)
        ship(c, S1, ph.at[c, turn(x, 2), pl.ds(0, 2)], r1h.at[c, 0], at_x(1))
        ship(c, S1 + 1, pg.at[c, turn(y, 2), pl.ds(0, 2)], r1g.at[c, 0], at_y(1))
        ship(c, S1 + 2, ph.at[c, turn(x, 2), pl.ds(2, 2)], r1h.at[c, 1], at_x(3))
        ship(c, S1 + 3, pg.at[c, turn(y, 2), pl.ds(2, 2)], r1g.at[c, 1], at_y(3))

    def add_first(c):
        land(c, S1, S2)

        def half(k, _):
            ph[c, turn(x, 1), k] += r1h[c, 0, k]
            pg[c, turn(y, 1), k] += r1g[c, 0, k]
            ph[c, turn(x, 3), 2 + k] += r1h[c, 1, k]
            pg[c, turn(y, 3), 2 + k] += r1g[c, 1, k]
            return 0

        lax.fori_loop(0, 2, half, 0)
        ship(c, S2, ph.at[c, turn(x, 1)], r2h.at[c, 0], at_x(1))
        ship(c, S2 + 1, pg.at[c, turn(y, 1)], r2g.at[c, 0], at_y(1))
        ship(c, S2 + 2, ph.at[c, turn(x, 3)], r2h.at[c, 1], at_x(3))
        ship(c, S2 + 3, pg.at[c, turn(y, 3)], r2g.at[c, 1], at_y(3))

    def add_second(c):
        land(c, S2, S3)

        def quarter(k, _):
            for own_part, come, total, at in ((ph, r2h, sh, x), (pg, r2g, sg, y)):
                total[c, k] = (
                    own_part[c, at, k].astype(F32) + come[c, 0, k].astype(F32) + come[c, 1, k].astype(F32)
                ).astype(BF16)
            return 0

        lax.fori_loop(0, SIDE, quarter, 0)
        for j in (1, 2, 3):
            ship(c, S3 + 2 * (j - 1), sh.at[c, turn(y, j)], r3h.at[c, j - 1], at_y(j))
            ship(c, S3 + 2 * (j - 1) + 1, sg.at[c, turn(x, j)], r3g.at[c, j - 1], at_x(j))

    def activate(c):
        land(c, S3, S4)

        def some_rows(i, _):
            rows = pl.ds(pl.multiple_of(i * ROWS, ROWS), ROWS)
            value, slope = sh[c, y, rows].astype(F32), sg[c, x, rows].astype(F32)
            for j in range(3):
                value += r3h[c, j, rows].astype(F32)
                slope += r3g[c, j, rows].astype(F32)
            root = 0.7978845608028654
            square = value * value
            tan = jnp.tanh(root * (value + 0.044715 * (square * value)))
            gate = 0.5 * (1.0 + tan)
            bend = 0.5 * value * (1.0 - tan * tan) * (root * (1.0 + 3.0 * 0.044715 * square))
            act[c, x, y, rows] = (value * gate).astype(BF16)
            grad[c, y, x, rows] = (slope * (gate + bend)).astype(BF16)
            return 0

        lax.fori_loop(0, BLK // ROWS, some_rows, 0)
        for j in (1, 2, 3):
            ship(c, S4 + 2 * (j - 1), act.at[c, x, y], act.at[c, x, y], at_y(j))
            ship(c, S4 + 2 * (j - 1) + 1, grad.at[c, y, x], grad.at[c, y, x], at_x(j))

    def spread_first(c):
        land(c, S4, S5)
        ship(c, S5, act.at[c, x], act.at[c, x], at_x(1))
        ship(c, S5 + 1, grad.at[c, y], grad.at[c, y], at_y(1))
        ship(c, S5 + 2, act.at[c, x], act.at[c, x], at_x(3))
        ship(c, S5 + 3, grad.at[c, y], grad.at[c, y], at_y(3))

    def spread_second(c):
        land(c, S5, S6)
        low, high = pl.ds(0, 2), pl.ds(2, 2)
        left, right, under, over = turn(x, 3), turn(x, 1), turn(y, 3), turn(y, 1)
        ship(c, S6, act.at[c, left, low], act.at[c, left, low], at_x(1))
        ship(c, S6 + 1, grad.at[c, under, low], grad.at[c, under, low], at_y(1))
        ship(c, S6 + 2, act.at[c, right, high], act.at[c, right, high], at_x(3))
        ship(c, S6 + 3, grad.at[c, over, high], grad.at[c, over, high], at_y(3))

    held = []

    def multiply_out(c):
        land(c, S6, S7)
        for k, (src, dst) in enumerate(((act, act_out), (grad, grad_out))):
            copy = pltpu.make_async_copy(src.at[c], dst.at[c], lsem.at[2 + 2 * c + k])
            copy.start()
            held.append(copy)

        def part(n, _):
            cols = pl.ds(pl.multiple_of(n * 256, 256), 256)
            out = jnp.zeros((TOK, 256), F32)
            gin = jnp.zeros((TOK, 256), F32)
            for q in range(SIDE):
                out += dot(act[c, :, q].reshape(TOK, QW), down[q, :, cols], 0)
                gin += dot(grad[c, q].reshape(TOK, QW), up[q, cols], 1)
            po[c, :, 0, :, cols] = out.astype(BF16).reshape(COLS, ROWS, 256)
            po[c, :, 1, :, cols] = gin.astype(BF16).reshape(COLS, ROWS, 256)
            return 0

        lax.fori_loop(0, FEAT // 256, part, 0)
        for j in range(1, COLS):
            ship(c, S7 + j - 1, po.at[c, col_of(j)], r7.at[c, j - 1], (row, col_of(j)))

    def finish(c):
        land(c, S7, SEMS)
        for k, out in enumerate((outputs, grad_inputs)):
            total = po[c, col, k].astype(F32)
            for j in range(COLS - 1):
                total += r7[c, j, k].astype(F32)
            out[c] = total.astype(BF16)

    stages = (multiply_in, add_first, add_second, activate, spread_first, spread_second, multiply_out, finish)
    for stage, c in ORDER:
        stages[stage](c)
        if (stage, c) == (0, CHUNKS - 1):
            copy = pltpu.make_async_copy(xin, x_out, lsem.at[0])
            copy.start()
            held.append(copy)
    for copy in held:
        copy.wait()
    for copy in copies.values():
        copy.wait_send()


def run_block(inputs, w_up, w_down, mask_up, mask_down, cotangent):
    vmem = pl.BlockSpec(memory_space=pltpu.VMEM)
    smem = pl.BlockSpec(memory_space=pltpu.SMEM)
    hbm = pl.BlockSpec(memory_space=pl.ANY)
    piece = (BLK, QW)

    def buf(*dims):
        return pltpu.VMEM((CHUNKS, *dims), BF16)

    return pl.pallas_call(
        block_kernel,
        out_shape=[
            jax.ShapeDtypeStruct((CHUNKS, ROWS, FEAT), BF16),
            jax.ShapeDtypeStruct((CHUNKS, ROWS, FEAT), BF16),
            jax.ShapeDtypeStruct((CHUNKS, COLS, 2, ROWS, FEAT), BF16),
            jax.ShapeDtypeStruct((CHUNKS, SIDE, SIDE, *piece), BF16),
            jax.ShapeDtypeStruct((CHUNKS, SIDE, SIDE, *piece), BF16),
        ],
        in_specs=[hbm, hbm, hbm, smem, smem, hbm],
        out_specs=[vmem, vmem, hbm, hbm, hbm],
        scratch_shapes=[
            buf(COLS, 2, ROWS, FEAT),
            pltpu.VMEM((SIDE, FEAT, QW), BF16),
            pltpu.VMEM((SIDE, QW, FEAT), BF16),
            buf(SIDE, SIDE, *piece),
            buf(SIDE, SIDE, *piece),
            buf(2, 2, *piece),
            buf(2, 2, *piece),
            buf(2, SIDE, *piece),
            buf(2, SIDE, *piece),
            buf(SIDE, *piece),
            buf(SIDE, *piece),
            buf(3, *piece),
            buf(3, *piece),
            buf(SIDE, SIDE, *piece),
            buf(SIDE, SIDE, *piece),
            buf(COLS, 2, ROWS, FEAT),
            buf(COLS - 1, 2, ROWS, FEAT),
            pltpu.SemaphoreType.DMA((CHUNKS, SEMS)),
            pltpu.SemaphoreType.DMA((CHUNKS, SEMS)),
            pltpu.SemaphoreType.DMA((2, SIDE)),
            pltpu.SemaphoreType.DMA((2 + 2 * CHUNKS,)),
        ],
        compiler_params=pltpu.CompilerParams(
            collective_id=0, has_side_effects=True, vmem_limit_bytes=56 * 2**20
        ),
    )(
        inputs.reshape(CHUNKS, ROWS, FEAT),
        w_up,
        w_down,
        mask_up,
        mask_down,
        cotangent.reshape(CHUNKS, ROWS, FEAT),
    )


def weight_kernel(x_ref, act_ref, grad_ref, mask_up, mask_down, gup, gdown):
    q = pl.program_id(0)
    tokens = CHUNKS * TOK
    ins = x_ref[:, :, 0].reshape(tokens, FEAT)
    cot = x_ref[:, :, 1].reshape(tokens, FEAT)
    acts = act_ref[...].reshape(tokens, QW)
    grads = grad_ref[...].reshape(tokens, QW)

    def tn(left, right):
        return lax.dot_general(left, right, (((0,), (0,)), ((), ())), preferred_element_type=F32)

    for i in range(SUB):
        rows = pl.ds(i * TILE, TILE)
        up = tn(ins[:, i * TILE : (i + 1) * TILE], grads)
        down = tn(acts[:, i * TILE : (i + 1) * TILE], cot)
        for j in range(SUB):
            cols = slice(j * TILE, (j + 1) * TILE)
            gup[rows, cols] = up[:, cols].astype(BF16) * mask_up[i, q * SUB + j].astype(F32).astype(BF16)
            gdown[rows, cols] = down[:, cols].astype(BF16) * mask_down[q * SUB + i, j].astype(F32).astype(BF16)


def weight_grads(x_all, act_all, grad_all, mask_up, mask_down):
    smem = pl.BlockSpec(memory_space=pltpu.SMEM)
    return pl.pallas_call(
        weight_kernel,
        grid=(SIDE,),
        out_shape=[
            jax.ShapeDtypeStruct((FEAT, SIDE * QW), BF16),
            jax.ShapeDtypeStruct((SIDE * QW, FEAT), BF16),
        ],
        in_specs=[
            pl.BlockSpec(x_all.shape, lambda q: (0,) * 5),
            pl.BlockSpec((CHUNKS, SIDE, 1, BLK, QW), lambda q: (0, 0, q, 0, 0)),
            pl.BlockSpec((CHUNKS, 1, SIDE, BLK, QW), lambda q: (0, q, 0, 0, 0)),
            smem,
            smem,
        ],
        out_specs=[pl.BlockSpec((FEAT, QW), lambda q: (0, q)), pl.BlockSpec((QW, FEAT), lambda q: (q, 0))],
        compiler_params=pltpu.CompilerParams(vmem_limit_bytes=40 * 2**20),
    )(x_all, act_all, grad_all, mask_up, mask_down)


def per_device(inputs, w_up, w_down, mask_up, mask_down, cotangent):
    outputs, grad_inputs, x_all, act_all, grad_all = run_block(
        inputs, w_up, w_down, mask_up, mask_down, cotangent
    )
    grad_up, grad_down = weight_grads(x_all, act_all, grad_all, mask_up, mask_down)
    return (outputs.reshape(inputs.shape), grad_inputs.reshape(inputs.shape), grad_up, grad_down)


def solution(mesh):
    in_specs = (
        P("col", "row"),
        P("row", "col"),
        P("col", "row"),
        P("row", "col"),
        P("col", "row"),
        P("col", "row"),
    )
    out_specs = (P("col", "row"), P("col", "row"), P("row", "col"), P("col", "row"))
    return jax.shard_map(
        per_device, mesh=mesh, in_specs=in_specs, out_specs=out_specs, check_vma=False
    )
```

```python
import functools

import jax
import jax.numpy as jnp
from jax import lax
from jax.experimental import pallas as pl
from jax.experimental.pallas import tpu as pltpu
from jax.sharding import PartitionSpec as P

MESH = pl.DeviceIdType.MESH
BF16 = jnp.bfloat16
F32 = jnp.float32
SIDE = 4
CHUNKS = 4
COLS = 8
ROWS = 16
TOK = COLS * ROWS
BLK = TOK // SIDE
FEAT = 768
QW = 768
TILE = 128
SUB = FEAT // TILE
S0, S1, S2, S3, S4, S5, S6, S7 = range(8)

ORDER = (
    (0, 0), (0, 1), (1, 0), (0, 2), (1, 1), (0, 3), (2, 0), (1, 2), (2, 1), (1, 3), (3, 0), (2, 2), (3, 1), (2, 3),
    (4, 0), (3, 2), (4, 1), (3, 3), (5, 0), (4, 2), (5, 1), (4, 3), (6, 0), (5, 2), (6, 1), (5, 3), (6, 2), (6, 3),
    (7, 0), (7, 1), (7, 2), (7, 3),
)


def dot(left, right, right_dim):
    return lax.dot_general(left, right, (((1,), (right_dim,)), ((), ())), preferred_element_type=F32)


def block_kernel(
    inputs, w_up, w_down, up_bits, down_bits, cotangent,
    outputs, grad_inputs, xin, xt, act_t, grad,
    up, down, ph, pg, r1h, r1g, r2h, r2g, sh, sg, r3h, r3g, act, po, r7, mask_up, mask_down,
    send, recv, wsem, lsem,
):
    row, col = lax.axis_index("row"), lax.axis_index("col")
    x, y = row // SIDE, lax.rem(row, SIDE)

    def turn(v, by):
        return lax.rem(v + by, SIDE)

    def at_x(by):
        return (turn(x, by) * SIDE + y, col)

    def at_y(by):
        return (x * SIDE + turn(y, by), col)

    def col_of(by):
        return lax.rem(col + by, COLS)

    barrier = pltpu.get_barrier_semaphore()
    partners = [at_x(j) for j in (1, 2, 3)] + [at_y(j) for j in (1, 2, 3)] + [(row, col_of(j)) for j in range(1, COLS)]
    for device in partners:
        pl.semaphore_signal(barrier, inc=1, device_id=device, device_id_type=MESH)

    own = [
        pltpu.make_async_copy(up_bits, mask_up, lsem.at[2]),
        pltpu.make_async_copy(down_bits, mask_down, lsem.at[3]),
        pltpu.make_async_copy(inputs, xin.at[:, col, 0], lsem.at[0]),
        pltpu.make_async_copy(cotangent, xin.at[:, col, 1], lsem.at[1]),
    ]
    for copy in own:
        copy.start()
    loads = []
    for q in range(SIDE):
        loads.append(
            (
                pltpu.make_async_copy(w_up.at[:, pl.ds(q * QW, QW)], up.at[q], wsem.at[0, q]),
                pltpu.make_async_copy(w_down.at[pl.ds(q * QW, QW)], down.at[q], wsem.at[1, q]),
            )
        )
    for pair in loads:
        for copy in pair:
            copy.start()
    for copy in own:
        copy.wait()
    pl.semaphore_wait(barrier, len(partners))

    def ship(c, step, src, dst, device):
        pltpu.make_async_remote_copy(
            src_ref=src,
            dst_ref=dst,
            send_sem=send.at[step],
            recv_sem=recv.at[c, step],
            device_id=device,
            device_id_type=MESH,
        ).start()

    def await_bytes(like, sem):
        pltpu.make_async_copy(like, like, sem).wait()

    def land(c, step):
        like = {S0: r7.at[c], S1: ph.at[c, pl.ds(0, 2)], S2: ph.at[c], S3: ph.at[c, pl.ds(0, 2), pl.ds(0, 3)]}
        like.update({S4: like[S3], S5: like[S2], S6: like[S1], S7: like[S0]})
        await_bytes(like[step], recv.at[c, step])

    def gather(c):
        for j in range(1, COLS):
            ship(c, S0, xin.at[c, col], xin.at[c, col], (row, col_of(j)))

    gather(0)

    def drop_tiles(q, _):
        def one_row(i, _):
            rows = pl.ds(pl.multiple_of(i * TILE, TILE), TILE)
            for j in range(SUB):
                cols = pl.ds(j * TILE, TILE)
                up[q, rows, cols] = up[q, rows, cols] * mask_up[i, q * SUB + j].astype(F32).astype(BF16)
                down[q, rows, cols] = down[q, rows, cols] * mask_down[j, q * SUB + i].astype(F32).astype(BF16)
            return 0

        return lax.fori_loop(0, SUB, one_row, 0)

    for q in range(SIDE):
        for copy in loads[q]:
            copy.wait()
        drop_tiles(q, 0)

    def multiply_in(c):
        land(c, S0)
        if c + 1 < CHUNKS:
            gather(c + 1)

        def ahead(q, _):
            ins = xin[c, :, 0].reshape(TOK, FEAT)
            ph[c, :, q] = dot(ins, up[q], 0).astype(BF16).reshape(SIDE, BLK, QW)
            return 0

        def back(k, _):
            q = turn(y, k)
            cot = xin[c, :, 1].reshape(TOK, FEAT)
            pg[c, q] = dot(cot, down[q], 1).astype(BF16).reshape(SIDE, BLK, QW)
            return 0

        lax.fori_loop(2, 3, back, 0)
        ship(c, S1, pg.at[c, turn(y, 2), pl.ds(0, 2)], r1g.at[c, 0], at_y(1))
        ship(c, S1, pg.at[c, turn(y, 2), pl.ds(2, 2)], r1g.at[c, 1], at_y(3))
        lax.fori_loop(0, 2, ahead, 0)
        ship(c, S1, ph.at[c, turn(x, 2), pl.ds(0, 2)], r1h.at[c, 0], at_x(1))
        lax.fori_loop(2, 4, ahead, 0)
        ship(c, S1, ph.at[c, turn(x, 2), pl.ds(2, 2)], r1h.at[c, 1], at_x(3))
        lax.fori_loop(3, 6, back, 0)

    def add_first(c):
        land(c, S1)

        def half(k, _):
            ph[c, turn(x, 1), k] += r1h[c, 0, k]
            pg[c, turn(y, 1), k] += r1g[c, 0, k]
            ph[c, turn(x, 3), 2 + k] += r1h[c, 1, k]
            pg[c, turn(y, 3), 2 + k] += r1g[c, 1, k]
            return 0

        lax.fori_loop(0, 2, half, 0)
        ship(c, S2, ph.at[c, turn(x, 1)], r2h.at[c, 0], at_x(1))
        ship(c, S2, pg.at[c, turn(y, 1)], r2g.at[c, 0], at_y(1))
        ship(c, S2, ph.at[c, turn(x, 3)], r2h.at[c, 1], at_x(3))
        ship(c, S2, pg.at[c, turn(y, 3)], r2g.at[c, 1], at_y(3))

    def add_second(c):
        land(c, S2)

        def quarter(k, _):
            for own_part, come, total, at in ((ph, r2h, sh, x), (pg, r2g, sg, y)):
                total[c, k] = (
                    own_part[c, at, k].astype(F32) + come[c, 0, k].astype(F32) + come[c, 1, k].astype(F32)
                ).astype(BF16)
            return 0

        lax.fori_loop(0, SIDE, quarter, 0)
        for j in (1, 2, 3):
            ship(c, S3, sh.at[c, turn(y, j)], r3h.at[c, j - 1], at_y(j))
            ship(c, S3, sg.at[c, turn(x, j)], r3g.at[c, j - 1], at_x(j))

    def activate(c):
        land(c, S3)

        def some_rows(i, _):
            rows = pl.ds(pl.multiple_of(i * ROWS, ROWS), ROWS)
            value, slope = sh[c, y, rows].astype(F32), sg[c, x, rows].astype(F32)
            for j in range(3):
                value += r3h[c, j, rows].astype(F32)
                slope += r3g[c, j, rows].astype(F32)
            root = 0.7978845608028654
            square = value * value
            tan = jnp.tanh(root * (value + 0.044715 * (square * value)))
            gate = 0.5 * (1.0 + tan)
            bend = 0.5 * value * (1.0 - tan * tan) * (root * (1.0 + 3.0 * 0.044715 * square))
            act[c, x, y, rows] = (value * gate).astype(BF16)
            grad[c, y, x, rows] = (slope * (gate + bend)).astype(BF16)
            return 0

        lax.fori_loop(0, BLK // ROWS, some_rows, 0)
        for j in (1, 2, 3):
            ship(c, S4, act.at[c, x, y], act.at[c, x, y], at_y(j))
            ship(c, S4, grad.at[c, y, x], grad.at[c, y, x], at_x(j))

    def spread_first(c):
        land(c, S4)
        ship(c, S5, act.at[c, x], act.at[c, x], at_x(1))
        ship(c, S5, grad.at[c, y], grad.at[c, y], at_y(1))
        ship(c, S5, act.at[c, x], act.at[c, x], at_x(3))
        ship(c, S5, grad.at[c, y], grad.at[c, y], at_y(3))

    def spread_second(c):
        land(c, S5)
        low, high = pl.ds(0, 2), pl.ds(2, 2)
        left, right, under, over = turn(x, 3), turn(x, 1), turn(y, 3), turn(y, 1)
        ship(c, S6, act.at[c, left, low], act.at[c, left, low], at_x(1))
        ship(c, S6, grad.at[c, under, low], grad.at[c, under, low], at_y(1))
        ship(c, S6, act.at[c, right, high], act.at[c, right, high], at_x(3))
        ship(c, S6, grad.at[c, over, high], grad.at[c, over, high], at_y(3))

    def multiply_out(c):
        land(c, S6)

        def out_part(n, _):
            cols = pl.ds(pl.multiple_of(n * 256, 256), 256)
            out = jnp.zeros((TOK, 256), F32)
            for q in range(SIDE):
                out += dot(act[c, :, q].reshape(TOK, QW), down[q, :, cols], 0)
            po[c, :, 0, :, cols] = out.astype(BF16).reshape(COLS, ROWS, 256)
            return 0

        def in_part(n, _):
            cols = pl.ds(pl.multiple_of(n * 256, 256), 256)
            out = jnp.zeros((TOK, 256), F32)
            for q in range(SIDE):
                out += dot(grad[c, q].reshape(TOK, QW), up[q, cols], 1)
            po[c, :, 1, :, cols] = out.astype(BF16).reshape(COLS, ROWS, 256)
            return 0

        lax.fori_loop(0, FEAT // 256, out_part, 0)
        for j in range(1, COLS):
            ship(c, S7, po.at[c, col_of(j), 0], r7.at[c, j - 1, 0], (row, col_of(j)))
        lax.fori_loop(0, FEAT // 256, in_part, 0)
        for j in range(1, COLS):
            ship(c, S7, po.at[c, col_of(j), 1], r7.at[c, j - 1, 1], (row, col_of(j)))
        here = slice(c * TOK, (c + 1) * TOK)

        def turned(q, _):
            act_t[q, :, here] = act[c, :, q].reshape(TOK, QW).T
            return 0

        lax.fori_loop(0, SIDE, turned, 0)
        xt[:, here] = xin[c, :, 0].reshape(TOK, FEAT).T

    def finish(c):
        land(c, S7)
        for k, out in enumerate((outputs, grad_inputs)):
            total = po[c, col, k].astype(F32)
            for j in range(COLS - 1):
                total += r7[c, j, k].astype(F32)
            out[c] = total.astype(BF16)

    stages = (multiply_in, add_first, add_second, activate, spread_first, spread_second, multiply_out, finish)
    for stage, c in ORDER:
        stages[stage](c)
    some = ph.at[:, pl.ds(0, 2), pl.ds(0, 3)]
    sent = {S0: r7, S1: ph.at[pl.ds(0, 2)], S2: ph, S3: some, S4: some, S5: ph, S6: ph.at[pl.ds(0, 2)], S7: r7}
    for step, like in sent.items():
        await_bytes(like, send.at[step])


def run_block(inputs, w_up, w_down, mask_up, mask_down, cotangent):
    vmem = pl.BlockSpec(memory_space=pltpu.VMEM)
    hbm = pl.BlockSpec(memory_space=pl.ANY)
    piece = (BLK, QW)

    def buf(*dims):
        return pltpu.VMEM((CHUNKS, *dims), BF16)

    return pl.pallas_call(
        block_kernel,
        out_shape=[
            buf(ROWS, FEAT),
            buf(ROWS, FEAT),
            buf(COLS, 2, ROWS, FEAT),
            pltpu.VMEM((FEAT, CHUNKS * TOK), BF16),
            pltpu.VMEM((SIDE, QW, CHUNKS * TOK), BF16),
            buf(SIDE, SIDE, *piece),
        ],
        in_specs=[hbm] * 6,
        out_specs=[vmem] * 6,
        scratch_shapes=[
            pltpu.VMEM((SIDE, FEAT, QW), BF16),
            pltpu.VMEM((SIDE, QW, FEAT), BF16),
            buf(SIDE, SIDE, *piece),
            buf(SIDE, SIDE, *piece),
            buf(2, 2, *piece),
            buf(2, 2, *piece),
            buf(2, SIDE, *piece),
            buf(2, SIDE, *piece),
            buf(SIDE, *piece),
            buf(SIDE, *piece),
            buf(3, *piece),
            buf(3, *piece),
            buf(SIDE, SIDE, *piece),
            buf(COLS, 2, ROWS, FEAT),
            buf(COLS - 1, 2, ROWS, FEAT),
            pltpu.SMEM((SUB, SIDE * SUB), jnp.int32),
            pltpu.SMEM((SUB, SIDE * SUB), jnp.int32),
            pltpu.SemaphoreType.DMA((8,)),
            pltpu.SemaphoreType.DMA((CHUNKS, 8)),
            pltpu.SemaphoreType.DMA((2, SIDE)),
            pltpu.SemaphoreType.DMA((4,)),
        ],
        compiler_params=pltpu.CompilerParams(
            collective_id=0, has_side_effects=True, vmem_limit_bytes=48 * 2**20
        ),
    )(
        inputs.reshape(CHUNKS, ROWS, FEAT),
        w_up,
        w_down,
        mask_up,
        mask_down.T,
        cotangent.reshape(CHUNKS, ROWS, FEAT),
    )


def weight_kernel(x_all, xt, act_t, grad, out_here, gin_here, mask_up, mask_down, outputs, grad_inputs, gup, gdown):
    step = pl.program_id(0)
    q, half = step // 2, lax.rem(step, 2)
    tokens = CHUNKS * TOK
    width = QW // 2
    first = pl.multiple_of(half * width, width)

    @pl.when(step == 0)
    def _():
        outputs[...] = out_here[...]
        grad_inputs[...] = gin_here[...]

    cot = x_all[:, :, 1].reshape(tokens, FEAT)
    grads = grad[:, q, :, :, pl.ds(first, width)].reshape(tokens, width)

    def up_rows(i, _):
        rows = pl.ds(pl.multiple_of(i * 256, 256), 256)
        up = dot(xt[rows], grads, 0)
        for k in range(2):
            for j in range(SUB // 2):
                cols = slice(j * TILE, (j + 1) * TILE)
                keep = mask_up[2 * i + k, step * (SUB // 2) + j].astype(F32).astype(BF16)
                gup[pl.ds(pl.multiple_of(i * 256 + k * TILE, TILE), TILE), cols] = (
                    up[k * TILE : (k + 1) * TILE, cols].astype(BF16) * keep
                )
        return 0

    lax.fori_loop(0, SUB // 2, up_rows, 0)

    def down_rows(i, _):
        here = pl.multiple_of(i * TILE, TILE)
        down = dot(act_t[q, pl.ds(pl.multiple_of(first + here, TILE), TILE)], cot, 0)
        for j in range(SUB):
            cols = slice(j * TILE, (j + 1) * TILE)
            keep = mask_down[j, step * (SUB // 2) + i].astype(F32).astype(BF16)
            gdown[pl.ds(here, TILE), cols] = down[:, cols].astype(BF16) * keep
        return 0

    lax.fori_loop(0, SUB // 2, down_rows, 0)


def weight_grads(x_all, xt, act_t, grad, outputs, grad_inputs, mask_up, mask_down):
    smem = pl.BlockSpec(memory_space=pltpu.SMEM)
    vmem = pl.BlockSpec(memory_space=pltpu.VMEM)
    width = QW // 2
    whole = pl.BlockSpec(outputs.shape, lambda s: (0, 0, 0))
    return pl.pallas_call(
        weight_kernel,
        grid=(2 * SIDE,),
        out_shape=[
            jax.ShapeDtypeStruct(outputs.shape, BF16),
            jax.ShapeDtypeStruct(outputs.shape, BF16),
            jax.ShapeDtypeStruct((FEAT, SIDE * QW), BF16),
            jax.ShapeDtypeStruct((SIDE * QW, FEAT), BF16),
        ],
        in_specs=[vmem] * 6 + [smem] * 2,
        out_specs=[
            whole,
            whole,
            pl.BlockSpec((FEAT, width), lambda s: (0, s)),
            pl.BlockSpec((width, FEAT), lambda s: (s, 0)),
        ],
        compiler_params=pltpu.CompilerParams(vmem_limit_bytes=24 * 2**20),
    )(x_all, xt, act_t, grad, outputs, grad_inputs, mask_up, mask_down.T)


def per_device(inputs, w_up, w_down, mask_up, mask_down, cotangent):
    kept = run_block(inputs, w_up, w_down, mask_up, mask_down, cotangent)
    outputs, grad_inputs, x_all, xt, act_t, grad = (
        pltpu.with_memory_space_constraint(array, pltpu.VMEM) for array in kept
    )
    outputs, grad_inputs, grad_up, grad_down = weight_grads(
        x_all, xt, act_t, grad, outputs, grad_inputs, mask_up, mask_down
    )
    return (outputs.reshape(inputs.shape), grad_inputs.reshape(inputs.shape), grad_up, grad_down)


def solution(mesh):
    in_specs = (
        P("col", "row"),
        P("row", "col"),
        P("col", "row"),
        P("row", "col"),
        P("col", "row"),
        P("col", "row"),
    )
    out_specs = (P("col", "row"), P("col", "row"), P("row", "col"), P("col", "row"))
    return jax.shard_map(
        per_device, mesh=mesh, in_specs=in_specs, out_specs=out_specs, check_vma=False
    )
```

```python
import functools

import jax
import jax.numpy as jnp
from jax import lax
from jax.experimental import pallas as pl
from jax.experimental.pallas import tpu as pltpu
from jax.sharding import PartitionSpec as P

MESH = pl.DeviceIdType.MESH
BF16 = jnp.bfloat16
F32 = jnp.float32
SIDE = 4
CHUNKS = 4
HALVES = 2
COLS = 8
ROWS = 16
TOK = COLS * ROWS
BLK = TOK // SIDE
FEAT = 768
QW = 384
TILE = 128
SUB = FEAT // TILE
Z0, K0, S1, S2, S3, S4, S5, S6, S7 = range(9)

ORDER = (
    (0, 0), (0, 1), (0, 2), (0, 3), (1, 0), (0, 4), (1, 1), (0, 5), (1, 2), (0, 6), (1, 3), (0, 7), (2, 0), (1, 4),
    (2, 1), (1, 5), (2, 2), (1, 6), (2, 3), (1, 7), (3, 0), (2, 4), (3, 1), (2, 5), (3, 2), (2, 6), (3, 3), (2, 7),
    (4, 0), (3, 4), (4, 1), (3, 5), (4, 2), (3, 6), (4, 3), (3, 7), (5, 0), (4, 4), (5, 1), (4, 5), (5, 2), (4, 6),
    (5, 3), (4, 7), (6, 0), (5, 4), (6, 1), (5, 5), (6, 2), (5, 6), (6, 3), (5, 7), (6, 4), (6, 5), (6, 6), (6, 7),
    (7, 1), (7, 3), (7, 5), (7, 7),
)


def beside(parts):
    return jnp.concatenate(parts, axis=1)


def dot(left, right, right_dim):
    return lax.dot_general(left, right, (((1,), (right_dim,)), ((), ())), preferred_element_type=F32)


def block_kernel(
    inputs, w_up, w_down, up_bits, down_bits, cotangent,
    outputs, grad_inputs, xin, xt, act_t, grad,
    up, down, ph, pg, r1h, r1g, r2h, r2g, sh, sg, r3h, r3g, act, acc, po, r7, mask_up, mask_down,
    send, recv, recv_col, wsem, lsem,
):
    row, col = lax.axis_index("row"), lax.axis_index("col")
    x, y = row // SIDE, lax.rem(row, SIDE)
    z, core = col // 2, lax.rem(col, 2)

    def turn(v, by):
        return lax.rem(v + by, SIDE)

    def at_x(by):
        return (turn(x, by) * SIDE + y, col)

    def at_y(by):
        return (x * SIDE + turn(y, by), col)

    def col_of(by):
        return lax.rem(col + by, COLS)

    barrier = pltpu.get_barrier_semaphore()
    partners = [at_x(j) for j in (1, 2, 3)] + [at_y(j) for j in (1, 2, 3)] + [(row, col_of(j)) for j in range(1, COLS)]
    for device in partners:
        pl.semaphore_signal(barrier, inc=1, device_id=device, device_id_type=MESH)

    own = [
        pltpu.make_async_copy(up_bits, mask_up, lsem.at[2]),
        pltpu.make_async_copy(down_bits, mask_down, lsem.at[3]),
        pltpu.make_async_copy(inputs, xin.at[:, col, 0], lsem.at[0]),
        pltpu.make_async_copy(cotangent, xin.at[:, col, 1], lsem.at[1]),
    ]
    for copy in own:
        copy.start()
    loads = []
    for b in range(SIDE):
        units = pl.ds(b * FEAT, FEAT)
        loads.append(
            (
                pltpu.make_async_copy(w_up.at[:, units], up.at[b], wsem.at[0, b]),
                pltpu.make_async_copy(w_down.at[units], down.at[b], wsem.at[1, b]),
            )
        )
    for pair in loads:
        for copy in pair:
            copy.start()
    for copy in own:
        copy.wait()
    pl.semaphore_wait(barrier, len(partners))

    def ship(step, landed, src, dst, device):
        pltpu.make_async_remote_copy(
            src_ref=src,
            dst_ref=dst,
            send_sem=send.at[step],
            recv_sem=landed,
            device_id=device,
            device_id_type=MESH,
        ).start()

    def await_bytes(like, sem):
        pltpu.make_async_copy(like, like, sem).wait()

    def land(c, f, step):
        some = ph.at[c, f, pl.ds(0, 2), pl.ds(0, 3)]
        like = {S1: ph.at[c, f, pl.ds(0, 2)], S2: ph.at[c, f], S3: some}
        like.update({S4: some, S5: like[S2], S6: like[S1]})
        await_bytes(like[step], recv.at[c, f, step - S1])

    sibling = (row, 2 * z + 1 - core)

    def gather_z(c):
        for j in (1, 2, 3):
            ship(Z0, recv_col.at[c, 0], xin.at[c, col], xin.at[c, col], (row, 2 * turn(z, j) + core))
        ship(K0, recv_col.at[c, 1], xin.at[c, col], xin.at[c, col], sibling)

    def gather_core(c):
        await_bytes(xin.at[c, pl.ds(0, 3)], recv_col.at[c, 0])
        for j in (1, 2, 3):
            there = 2 * turn(z, j) + core
            ship(K0, recv_col.at[c, 1], xin.at[c, there], xin.at[c, there], sibling)
        if c + 2 < CHUNKS:
            gather_z(c + 2)

    gather_z(0)

    def drop_tiles(q, _):
        def one_row(i, _):
            rows = pl.ds(pl.multiple_of(i * TILE, TILE), TILE)
            for j in range(SUB):
                cols = pl.ds(j * TILE, TILE)
                up[q, rows, cols] = up[q, rows, cols] * mask_up[i, q * SUB + j].astype(F32).astype(BF16)
                down[q, rows, cols] = down[q, rows, cols] * mask_down[j, q * SUB + i].astype(F32).astype(BF16)
            return 0

        return lax.fori_loop(0, SUB, one_row, 0)

    for b in range(SIDE):
        for copy in loads[b]:
            copy.wait()
        drop_tiles(b, 0)
        if b == 1:
            gather_z(1)
    gather_core(0)

    def multiply_in(c, f):
        if f == 0:
            await_bytes(xin.at[c, pl.ds(0, SIDE)], recv_col.at[c, 1])

        def ahead(n, _):
            ins = xin[c, :, 0].reshape(TOK, FEAT)
            wide = dot(ins, up[HALVES * f + n], 0).astype(BF16)
            for k in range(2):
                ph[c, f, :, 2 * n + k] = wide[:, k * QW : (k + 1) * QW].reshape(SIDE, BLK, QW)
            return 0

        def back(k, _):
            n = lax.rem(y // 2 + k, 2)
            cot = xin[c, :, 1].reshape(TOK, FEAT)
            wide = dot(cot, down[HALVES * f + n], 1).astype(BF16)
            for k in range(2):
                pg[c, f, 2 * n + k] = wide[:, k * QW : (k + 1) * QW].reshape(SIDE, BLK, QW)
            return 0

        landed = recv.at[c, f, 0]
        low, high = pl.ds(0, 2), pl.ds(2, 2)
        lax.fori_loop(1, 2, back, 0)
        ship(S1, landed, pg.at[c, f, turn(y, 2), low], r1g.at[c, f, 0], at_y(1))
        ship(S1, landed, pg.at[c, f, turn(y, 2), high], r1g.at[c, f, 1], at_y(3))
        lax.fori_loop(0, 1, ahead, 0)
        ship(S1, landed, ph.at[c, f, turn(x, 2), low], r1h.at[c, f, 0], at_x(1))
        lax.fori_loop(1, 2, ahead, 0)
        ship(S1, landed, ph.at[c, f, turn(x, 2), high], r1h.at[c, f, 1], at_x(3))
        lax.fori_loop(2, 3, back, 0)
        if f == 0 and c + 1 < CHUNKS:
            gather_core(c + 1)
        if f == 1:
            xt[:, c * TOK : (c + 1) * TOK] = xin[c, :, 0].reshape(TOK, FEAT).T

    def add_first(c, f):
        land(c, f, S1)

        def half(k, _):
            ph[c, f, turn(x, 1), k] += r1h[c, f, 0, k]
            pg[c, f, turn(y, 1), k] += r1g[c, f, 0, k]
            ph[c, f, turn(x, 3), 2 + k] += r1h[c, f, 1, k]
            pg[c, f, turn(y, 3), 2 + k] += r1g[c, f, 1, k]
            return 0

        lax.fori_loop(0, 2, half, 0)
        landed = recv.at[c, f, S2 - S1]
        ship(S2, landed, ph.at[c, f, turn(x, 1)], r2h.at[c, f, 0], at_x(1))
        ship(S2, landed, pg.at[c, f, turn(y, 1)], r2g.at[c, f, 0], at_y(1))
        ship(S2, landed, ph.at[c, f, turn(x, 3)], r2h.at[c, f, 1], at_x(3))
        ship(S2, landed, pg.at[c, f, turn(y, 3)], r2g.at[c, f, 1], at_y(3))

    def add_second(c, f):
        land(c, f, S2)

        def quarter(k, _):
            for own_part, come, total, at in ((ph, r2h, sh, x), (pg, r2g, sg, y)):
                total[c, f, k] = (
                    own_part[c, f, at, k].astype(F32) + come[c, f, 0, k].astype(F32) + come[c, f, 1, k].astype(F32)
                ).astype(BF16)
            return 0

        lax.fori_loop(0, SIDE, quarter, 0)
        landed = recv.at[c, f, S3 - S1]
        for j in (1, 2, 3):
            ship(S3, landed, sh.at[c, f, turn(y, j)], r3h.at[c, f, j - 1], at_y(j))
            ship(S3, landed, sg.at[c, f, turn(x, j)], r3g.at[c, f, j - 1], at_x(j))

    def activate(c, f):
        land(c, f, S3)

        def some_rows(i, _):
            rows = pl.ds(pl.multiple_of(i * ROWS, ROWS), ROWS)
            value, slope = sh[c, f, y, rows].astype(F32), sg[c, f, x, rows].astype(F32)
            for j in range(3):
                value += r3h[c, f, j, rows].astype(F32)
                slope += r3g[c, f, j, rows].astype(F32)
            root = 0.7978845608028654
            square = value * value
            tan = jnp.tanh(root * (value + 0.044715 * (square * value)))
            gate = 0.5 * (1.0 + tan)
            bend = 0.5 * value * (1.0 - tan * tan) * (root * (1.0 + 3.0 * 0.044715 * square))
            act[c, f, x, y, rows] = (value * gate).astype(BF16)
            grad[c, f, y, x, rows] = (slope * (gate + bend)).astype(BF16)
            return 0

        lax.fori_loop(0, BLK // ROWS, some_rows, 0)
        landed = recv.at[c, f, S4 - S1]
        for j in (1, 2, 3):
            ship(S4, landed, act.at[c, f, x, y], act.at[c, f, x, y], at_y(j))
            ship(S4, landed, grad.at[c, f, y, x], grad.at[c, f, y, x], at_x(j))

    def spread_first(c, f):
        land(c, f, S4)
        landed = recv.at[c, f, S5 - S1]
        for j in (1, 3):
            ship(S5, landed, act.at[c, f, x], act.at[c, f, x], at_x(j))
            ship(S5, landed, grad.at[c, f, y], grad.at[c, f, y], at_y(j))

    def spread_second(c, f):
        land(c, f, S5)
        low, high = pl.ds(0, 2), pl.ds(2, 2)
        landed = recv.at[c, f, S6 - S1]
        left, right, under, over = turn(x, 3), turn(x, 1), turn(y, 3), turn(y, 1)
        ship(S6, landed, act.at[c, f, left, low], act.at[c, f, left, low], at_x(1))
        ship(S6, landed, grad.at[c, f, under, low], grad.at[c, f, under, low], at_y(1))
        ship(S6, landed, act.at[c, f, right, high], act.at[c, f, right, high], at_x(3))
        ship(S6, landed, grad.at[c, f, over, high], grad.at[c, f, over, high], at_y(3))

    def multiply_out(c, f):
        land(c, f, S6)

        def some_columns(k, n):
            cols = pl.ds(pl.multiple_of(n * 256, 256), 256)
            out = jnp.zeros((TOK, 256), F32)
            for h in range(2):
                quarters = (2 * h, 2 * h + 1)
                if k == 0:
                    left = beside([act[c, f, :, q].reshape(TOK, QW) for q in quarters])
                    out += dot(left, down[HALVES * f + h, :, cols], 0)
                else:
                    left = beside([grad[c, f, q].reshape(TOK, QW) for q in quarters])
                    out += dot(left, up[HALVES * f + h, cols], 1)
            if f == 0:
                acc[c, k, :, cols] = out
            else:
                out += acc[c, k, :, cols]
                po[c, :, k, :, cols] = out.astype(BF16).reshape(COLS, ROWS, 256)

        for k in range(2):

            def some(n, _):
                some_columns(k, n)
                return 0

            lax.fori_loop(0, FEAT // 256, some, 0)
            if f == 1:
                for j in range(1, COLS):
                    there = col_of(j)
                    ship(S7, recv_col.at[c, 2], po.at[c, there, k], r7.at[c, j - 1, k], (row, there))

        def turned(q, _):
            rows = pl.ds(pl.multiple_of(lax.rem(q, 2) * QW, TILE), QW)
            act_t[HALVES * f + q // 2, rows, c * TOK : (c + 1) * TOK] = act[c, f, :, q].reshape(TOK, QW).T
            return 0

        lax.fori_loop(0, SIDE, turned, 0)

    def finish(c, _):
        await_bytes(r7.at[c], recv_col.at[c, 2])
        for k, out in enumerate((outputs, grad_inputs)):
            total = po[c, col, k].astype(F32)
            for j in range(COLS - 1):
                total += r7[c, j, k].astype(F32)
            out[c] = total.astype(BF16)

    stages = (multiply_in, add_first, add_second, activate, spread_first, spread_second, multiply_out, finish)
    for stage, part in ORDER:
        stages[stage](part // HALVES, part % HALVES)
    half, some = ph.at[pl.ds(0, 2)], ph.at[:, :, pl.ds(0, 2), pl.ds(0, 3)]
    sent = {Z0: xin.at[:, pl.ds(0, 3)], K0: xin.at[:, pl.ds(0, 4)], S1: half, S2: ph, S3: some, S4: some, S5: ph, S6: half}
    sent[S7] = r7
    for step, like in sent.items():
        await_bytes(like, send.at[step])


def run_block(inputs, w_up, w_down, mask_up, mask_down, cotangent):
    vmem = pl.BlockSpec(memory_space=pltpu.VMEM)
    hbm = pl.BlockSpec(memory_space=pl.ANY)

    def buf(*dims):
        return pltpu.VMEM((CHUNKS, *dims), BF16)

    def part(*dims):
        return buf(HALVES, *dims, BLK, QW)

    return pl.pallas_call(
        block_kernel,
        out_shape=[
            buf(ROWS, FEAT),
            buf(ROWS, FEAT),
            buf(COLS, 2, ROWS, FEAT),
            pltpu.VMEM((FEAT, CHUNKS * TOK), BF16),
            pltpu.VMEM((SIDE, FEAT, CHUNKS * TOK), BF16),
            part(SIDE, SIDE),
        ],
        in_specs=[hbm] * 6,
        out_specs=[vmem] * 6,
        scratch_shapes=[
            pltpu.VMEM((SIDE, FEAT, FEAT), BF16),
            pltpu.VMEM((SIDE, FEAT, FEAT), BF16),
            part(SIDE, SIDE),
            part(SIDE, SIDE),
            part(2, 2),
            part(2, 2),
            part(2, SIDE),
            part(2, SIDE),
            part(SIDE),
            part(SIDE),
            part(3),
            part(3),
            part(SIDE, SIDE),
            pltpu.VMEM((CHUNKS, 2, TOK, FEAT), F32),
            buf(COLS, 2, ROWS, FEAT),
            buf(COLS - 1, 2, ROWS, FEAT),
            pltpu.SMEM((SUB, SIDE * SUB), jnp.int32),
            pltpu.SMEM((SUB, SIDE * SUB), jnp.int32),
            pltpu.SemaphoreType.DMA((9,)),
            pltpu.SemaphoreType.DMA((CHUNKS, HALVES, 6)),
            pltpu.SemaphoreType.DMA((CHUNKS, 3)),
            pltpu.SemaphoreType.DMA((2, SIDE)),
            pltpu.SemaphoreType.DMA((4,)),
        ],
        compiler_params=pltpu.CompilerParams(
            collective_id=0, has_side_effects=True, vmem_limit_bytes=48 * 2**20
        ),
    )(
        inputs.reshape(CHUNKS, ROWS, FEAT),
        w_up,
        w_down,
        mask_up,
        mask_down.T,
        cotangent.reshape(CHUNKS, ROWS, FEAT),
    )


def weight_kernel(
    x_all, xt, act_t, grad, out_here, gin_here, up_bits, down_bits, outputs, grad_inputs, gup, gdown,
    stage_up, stage_down, mask_up, mask_down, sems,
):
    tokens = CHUNKS * TOK
    bits = [
        pltpu.make_async_copy(up_bits, mask_up, sems.at[0]),
        pltpu.make_async_copy(down_bits, mask_down, sems.at[1]),
    ]
    moves = [
        pltpu.make_async_copy(out_here, outputs, sems.at[2]),
        pltpu.make_async_copy(gin_here, grad_inputs, sems.at[3]),
    ]
    for copy in bits + moves:
        copy.start()
    for b in range(SIDE):
        f, h = b // 2, b % 2
        units = pl.ds(b * FEAT, FEAT)
        grads = beside([grad[:, f, 2 * h + k].reshape(tokens, QW) for k in range(2)])
        for up in (True, False):
            if up:
                wide = dot(xt[...], grads, 0)
            else:
                wide = dot(act_t[b], x_all[:, :, 1].reshape(tokens, FEAT), 0)
            if b == 0 and up:
                for copy in bits:
                    copy.wait()
            stage = stage_up if up else stage_down
            for i in range(SUB):
                for j in range(SUB):
                    keep = mask_up[i, b * SUB + j] if up else mask_down[j, b * SUB + i]
                    rows, cols = slice(i * TILE, (i + 1) * TILE), slice(j * TILE, (j + 1) * TILE)
                    stage[b, rows, cols] = (wide[rows, cols] * keep.astype(F32)).astype(BF16)
            if up:
                copy = pltpu.make_async_copy(stage.at[b], gup.at[:, units], sems.at[4 + 2 * b])
            else:
                copy = pltpu.make_async_copy(stage.at[b], gdown.at[units], sems.at[5 + 2 * b])
            copy.start()
            moves.append(copy)
    for copy in moves:
        copy.wait()


def weight_grads(x_all, xt, act_t, grad, outputs, grad_inputs, mask_up, mask_down):
    vmem = pl.BlockSpec(memory_space=pltpu.VMEM)
    hbm = pl.BlockSpec(memory_space=pl.ANY)
    return pl.pallas_call(
        weight_kernel,
        out_shape=[
            jax.ShapeDtypeStruct(outputs.shape, BF16),
            jax.ShapeDtypeStruct(outputs.shape, BF16),
            jax.ShapeDtypeStruct((FEAT, SIDE * FEAT), BF16),
            jax.ShapeDtypeStruct((SIDE * FEAT, FEAT), BF16),
        ],
        in_specs=[vmem] * 6 + [hbm] * 2,
        out_specs=[hbm] * 4,
        scratch_shapes=[
            pltpu.VMEM((SIDE, FEAT, FEAT), BF16),
            pltpu.VMEM((SIDE, FEAT, FEAT), BF16),
            pltpu.SMEM((SUB, SIDE * SUB), jnp.int32),
            pltpu.SMEM((SUB, SIDE * SUB), jnp.int32),
            pltpu.SemaphoreType.DMA((4 + 2 * SIDE,)),
        ],
        compiler_params=pltpu.CompilerParams(vmem_limit_bytes=24 * 2**20),
    )(x_all, xt, act_t, grad, outputs, grad_inputs, mask_up, mask_down.T)


def per_device(inputs, w_up, w_down, mask_up, mask_down, cotangent):
    kept = run_block(inputs, w_up, w_down, mask_up, mask_down, cotangent)
    outputs, grad_inputs, x_all, xt, act_t, grad = (
        pltpu.with_memory_space_constraint(array, pltpu.VMEM) for array in kept
    )
    outputs, grad_inputs, grad_up, grad_down = weight_grads(
        x_all, xt, act_t, grad, outputs, grad_inputs, mask_up, mask_down
    )
    return (outputs.reshape(inputs.shape), grad_inputs.reshape(inputs.shape), grad_up, grad_down)


def solution(mesh):
    in_specs = (
        P("col", "row"),
        P("row", "col"),
        P("col", "row"),
        P("row", "col"),
        P("col", "row"),
        P("col", "row"),
    )
    out_specs = (P("col", "row"), P("col", "row"), P("row", "col"), P("col", "row"))
    return jax.shard_map(
        per_device, mesh=mesh, in_specs=in_specs, out_specs=out_specs, check_vma=False
    )
```

```python
import functools

import jax
import jax.numpy as jnp
from jax import lax
from jax.experimental import pallas as pl
from jax.experimental.pallas import tpu as pltpu
from jax.sharding import PartitionSpec as P

MESH = pl.DeviceIdType.MESH
BF16 = jnp.bfloat16
F32 = jnp.float32
SIDE = 4
CHUNKS = 4
HALVES = 2
COLS = 8
ROWS = 16
TOK = COLS * ROWS
BLK = TOK // SIDE
FEAT = 768
QW = 384
TILE = 128
SUB = FEAT // TILE
Z0, K0, S1, S2, S3, S4, S5, S6, S7, S8, S9 = range(11)

ORDER = (
    (0, 0), (0, 1), (0, 2), (0, 3), (1, 0), (0, 4), (1, 1), (0, 5), (1, 2), (1, 3), (0, 6), (0, 7), (2, 0), (1, 4),
    (2, 1), (1, 5), (2, 2), (2, 3), (1, 6), (1, 7), (3, 0), (2, 4), (3, 1), (2, 5), (3, 2), (3, 3), (2, 6), (2, 7),
    (4, 0), (3, 4), (4, 1), (3, 5), (4, 2), (4, 3), (3, 6), (3, 7), (5, 0), (4, 4), (5, 1), (4, 5), (5, 2), (5, 3),
    (4, 6), (4, 7), (6, 0), (5, 4), (6, 1), (5, 5), (6, 2), (6, 3), (5, 6), (5, 7), (7, 0), (6, 4), (7, 1), (6, 5),
    (7, 2), (7, 3), (6, 6), (6, 7), (8, 0), (7, 4), (8, 1), (7, 5), (8, 2), (8, 3), (7, 6), (7, 7), (8, 4), (8, 5),
    (8, 6), (8, 7), (9, 1), (9, 3), (9, 5), (9, 7),
)


def beside(parts):
    return jnp.concatenate(parts, axis=1)


def dot(left, right, right_dim):
    return lax.dot_general(left, right, (((1,), (right_dim,)), ((), ())), preferred_element_type=F32)


def block_kernel(
    inputs, w_up, w_down, up_bits, down_bits, cotangent,
    outputs, grad_inputs, up, down,
    xin, xt, act_t, grad, ph, pg, r1h, r1g, r2h, r2g, sh, sg, r3h, r3g, r4h, r4g, act, acc, po, r9, mask_up, mask_down,
    send, recv, recv_col, wsem, lsem,
):
    row, col = lax.axis_index("row"), lax.axis_index("col")
    x, y = row // SIDE, lax.rem(row, SIDE)
    z, core = col // 2, lax.rem(col, 2)

    def turn(v, by):
        return lax.rem(v + by, SIDE)

    def at_x(by):
        return (turn(x, by) * SIDE + y, col)

    def at_y(by):
        return (x * SIDE + turn(y, by), col)

    def col_of(by):
        return lax.rem(col + by, COLS)

    barrier = pltpu.get_barrier_semaphore()
    partners = [at_x(j) for j in (1, 2, 3)] + [at_y(j) for j in (1, 2, 3)] + [(row, col_of(j)) for j in range(1, COLS)]
    for device in partners:
        pl.semaphore_signal(barrier, inc=1, device_id=device, device_id_type=MESH)

    own = [
        pltpu.make_async_copy(up_bits, mask_up, lsem.at[2]),
        pltpu.make_async_copy(down_bits, mask_down, lsem.at[3]),
        pltpu.make_async_copy(inputs, xin.at[:, col, 0], lsem.at[0]),
        pltpu.make_async_copy(cotangent, xin.at[:, col, 1], lsem.at[1]),
    ]
    for copy in own:
        copy.start()
    loads = []
    for b in range(SIDE):
        units = pl.ds(b * FEAT, FEAT)
        loads.append(
            (
                pltpu.make_async_copy(w_up.at[:, units], up.at[b], wsem.at[0, b]),
                pltpu.make_async_copy(w_down.at[units], down.at[b], wsem.at[1, b]),
            )
        )
    for pair in loads:
        for copy in pair:
            copy.start()
    for copy in own:
        copy.wait()
    pl.semaphore_wait(barrier, len(partners))

    def ship(step, landed, src, dst, device):
        pltpu.make_async_remote_copy(
            src_ref=src,
            dst_ref=dst,
            send_sem=send.at[step],
            recv_sem=landed,
            device_id=device,
            device_id_type=MESH,
        ).start()

    def await_bytes(like, sem):
        pltpu.make_async_copy(like, like, sem).wait()

    def land(c, f, step):
        like = {S1: ph.at[c, f, pl.ds(0, 2)], S2: ph.at[c, f], S3: ph.at[c, f, 0, pl.ds(0, 2)], S4: ph.at[c, f, 0]}
        like.update({S5: like[S4], S6: like[S3], S7: like[S2], S8: like[S1]})
        await_bytes(like[step], recv.at[c, f, step - S1])

    sibling = (row, 2 * z + 1 - core)

    def gather_z(c):
        for j in (1, 2, 3):
            ship(Z0, recv_col.at[c, 0], xin.at[c, col], xin.at[c, col], (row, 2 * turn(z, j) + core))
        ship(K0, recv_col.at[c, 1], xin.at[c, col], xin.at[c, col], sibling)

    def gather_core(c):
        await_bytes(xin.at[c, pl.ds(0, 3)], recv_col.at[c, 0])
        for j in (1, 2, 3):
            there = 2 * turn(z, j) + core
            ship(K0, recv_col.at[c, 1], xin.at[c, there], xin.at[c, there], sibling)
        if c + 2 < CHUNKS:
            gather_z(c + 2)

    gather_z(0)

    def drop_tiles(q, _):
        def one_row(i, _):
            rows = pl.ds(pl.multiple_of(i * TILE, TILE), TILE)
            for j in range(SUB):
                cols = pl.ds(j * TILE, TILE)
                up[q, rows, cols] = up[q, rows, cols] * mask_up[i, q * SUB + j].astype(F32).astype(BF16)
                down[q, rows, cols] = down[q, rows, cols] * mask_down[j, q * SUB + i].astype(F32).astype(BF16)
            return 0

        return lax.fori_loop(0, SUB, one_row, 0)

    for b in range(SIDE):
        for copy in loads[b]:
            copy.wait()
        drop_tiles(b, 0)
        if b == 1:
            gather_z(1)
    gather_core(0)

    def multiply_in(c, f):
        if f == 0:
            await_bytes(xin.at[c, pl.ds(0, SIDE)], recv_col.at[c, 1])

        def ahead(n, _):
            ins = xin[c, :, 0].reshape(TOK, FEAT)
            wide = dot(ins, up[HALVES * f + n], 0).astype(BF16)
            for k in range(2):
                ph[c, f, :, 2 * n + k] = wide[:, k * QW : (k + 1) * QW].reshape(SIDE, BLK, QW)
            return 0

        def back(k, _):
            n = lax.rem(y // 2 + k, 2)
            cot = xin[c, :, 1].reshape(TOK, FEAT)
            wide = dot(cot, down[HALVES * f + n], 1).astype(BF16)
            for k in range(2):
                pg[c, f, 2 * n + k] = wide[:, k * QW : (k + 1) * QW].reshape(SIDE, BLK, QW)
            return 0

        landed = recv.at[c, f, 0]
        low, high = pl.ds(0, 2), pl.ds(2, 2)
        lax.fori_loop(1, 2, back, 0)
        ship(S1, landed, pg.at[c, f, turn(y, 2), low], r1g.at[c, f, 0], at_y(1))
        ship(S1, landed, pg.at[c, f, turn(y, 2), high], r1g.at[c, f, 1], at_y(3))
        lax.fori_loop(0, 1, ahead, 0)
        ship(S1, landed, ph.at[c, f, turn(x, 2), low], r1h.at[c, f, 0], at_x(1))
        lax.fori_loop(1, 2, ahead, 0)
        ship(S1, landed, ph.at[c, f, turn(x, 2), high], r1h.at[c, f, 1], at_x(3))
        lax.fori_loop(2, 3, back, 0)
        if f == 0 and c + 1 < CHUNKS:
            gather_core(c + 1)
        if f == 1:
            xt[:, c * TOK : (c + 1) * TOK] = xin[c, :, 0].reshape(TOK, FEAT).T

    def add_first(c, f):
        land(c, f, S1)

        def half(k, _):
            ph[c, f, turn(x, 1), k] += r1h[c, f, 0, k]
            pg[c, f, turn(y, 1), k] += r1g[c, f, 0, k]
            ph[c, f, turn(x, 3), 2 + k] += r1h[c, f, 1, k]
            pg[c, f, turn(y, 3), 2 + k] += r1g[c, f, 1, k]
            return 0

        lax.fori_loop(0, 2, half, 0)
        landed = recv.at[c, f, S2 - S1]
        ship(S2, landed, ph.at[c, f, turn(x, 1)], r2h.at[c, f, 0], at_x(1))
        ship(S2, landed, pg.at[c, f, turn(y, 1)], r2g.at[c, f, 0], at_y(1))
        ship(S2, landed, ph.at[c, f, turn(x, 3)], r2h.at[c, f, 1], at_x(3))
        ship(S2, landed, pg.at[c, f, turn(y, 3)], r2g.at[c, f, 1], at_y(3))

    def add_second(c, f):
        land(c, f, S2)

        def quarter(k, _):
            for own_part, come, total, at in ((ph, r2h, sh, x), (pg, r2g, sg, y)):
                total[c, f, k] = (
                    own_part[c, f, at, k].astype(F32) + come[c, f, 0, k].astype(F32) + come[c, f, 1, k].astype(F32)
                ).astype(BF16)
            return 0

        lax.fori_loop(0, SIDE, quarter, 0)
        landed = recv.at[c, f, S3 - S1]
        low, high = pl.ds(0, ROWS), pl.ds(ROWS, ROWS)
        ship(S3, landed, sh.at[c, f, turn(y, 2), low], r3h.at[c, f, 0], at_y(1))
        ship(S3, landed, sg.at[c, f, turn(x, 2), low], r3g.at[c, f, 0], at_x(1))
        ship(S3, landed, sh.at[c, f, turn(y, 2), high], r3h.at[c, f, 1], at_y(3))
        ship(S3, landed, sg.at[c, f, turn(x, 2), high], r3g.at[c, f, 1], at_x(3))

    def add_third(c, f):
        land(c, f, S3)
        low, high = pl.ds(0, ROWS), pl.ds(ROWS, ROWS)
        for total, come, at in ((sh, r3h, y), (sg, r3g, x)):
            total[c, f, turn(at, 1), low] += come[c, f, 0]
            total[c, f, turn(at, 3), high] += come[c, f, 1]
        landed = recv.at[c, f, S4 - S1]
        ship(S4, landed, sh.at[c, f, turn(y, 1)], r4h.at[c, f, 0], at_y(1))
        ship(S4, landed, sg.at[c, f, turn(x, 1)], r4g.at[c, f, 0], at_x(1))
        ship(S4, landed, sh.at[c, f, turn(y, 3)], r4h.at[c, f, 1], at_y(3))
        ship(S4, landed, sg.at[c, f, turn(x, 3)], r4g.at[c, f, 1], at_x(3))

    def activate(c, f):
        land(c, f, S4)

        def some_rows(i, _):
            rows = pl.ds(pl.multiple_of(i * ROWS, ROWS), ROWS)
            value, slope = sh[c, f, y, rows].astype(F32), sg[c, f, x, rows].astype(F32)
            for j in range(2):
                value += r4h[c, f, j, rows].astype(F32)
                slope += r4g[c, f, j, rows].astype(F32)
            root = 0.7978845608028654
            square = value * value
            tan = jnp.tanh(root * (value + 0.044715 * (square * value)))
            gate = 0.5 * (1.0 + tan)
            bend = 0.5 * value * (1.0 - tan * tan) * (root * (1.0 + 3.0 * 0.044715 * square))
            act[c, f, x, y, rows] = (value * gate).astype(BF16)
            grad[c, f, y, x, rows] = (slope * (gate + bend)).astype(BF16)
            return 0

        lax.fori_loop(0, BLK // ROWS, some_rows, 0)
        landed = recv.at[c, f, S5 - S1]
        for j in (1, 3):
            ship(S5, landed, act.at[c, f, x, y], act.at[c, f, x, y], at_y(j))
            ship(S5, landed, grad.at[c, f, y, x], grad.at[c, f, y, x], at_x(j))

    def spread_first(c, f):
        land(c, f, S5)
        low, high = pl.ds(0, ROWS), pl.ds(ROWS, ROWS)
        landed = recv.at[c, f, S6 - S1]
        left, right, under, over = turn(x, 3), turn(x, 1), turn(y, 3), turn(y, 1)
        ship(S6, landed, act.at[c, f, x, under, low], act.at[c, f, x, under, low], at_y(1))
        ship(S6, landed, grad.at[c, f, y, left, low], grad.at[c, f, y, left, low], at_x(1))
        ship(S6, landed, act.at[c, f, x, over, high], act.at[c, f, x, over, high], at_y(3))
        ship(S6, landed, grad.at[c, f, y, right, high], grad.at[c, f, y, right, high], at_x(3))

    def spread_second(c, f):
        land(c, f, S6)
        landed = recv.at[c, f, S7 - S1]
        for j in (1, 3):
            ship(S7, landed, act.at[c, f, x], act.at[c, f, x], at_x(j))
            ship(S7, landed, grad.at[c, f, y], grad.at[c, f, y], at_y(j))

    def spread_third(c, f):
        land(c, f, S7)
        low, high = pl.ds(0, 2), pl.ds(2, 2)
        landed = recv.at[c, f, S8 - S1]
        left, right, under, over = turn(x, 3), turn(x, 1), turn(y, 3), turn(y, 1)
        ship(S8, landed, act.at[c, f, left, low], act.at[c, f, left, low], at_x(1))
        ship(S8, landed, grad.at[c, f, under, low], grad.at[c, f, under, low], at_y(1))
        ship(S8, landed, act.at[c, f, right, high], act.at[c, f, right, high], at_x(3))
        ship(S8, landed, grad.at[c, f, over, high], grad.at[c, f, over, high], at_y(3))

    def multiply_out(c, f):
        land(c, f, S8)
        for k in range(2):
            out = acc[c, k] if f else jnp.zeros((TOK, FEAT), F32)
            for h in range(2):
                b, quarters = HALVES * f + h, (2 * h, 2 * h + 1)
                if k == 0:
                    left = beside([act[c, f, :, q].reshape(TOK, QW) for q in quarters])
                    out += dot(left, down[b], 0)
                else:
                    left = beside([grad[c, f, q].reshape(TOK, QW) for q in quarters])
                    out += dot(left, up[b], 1)
            if f == 0:
                acc[c, k] = out
            else:
                po[c, :, k] = out.astype(BF16).reshape(COLS, ROWS, FEAT)
                for j in range(1, COLS):
                    there = col_of(j)
                    ship(S9, recv_col.at[c, 2], po.at[c, there, k], r9.at[c, j - 1, k], (row, there))

        def turned(q, _):
            rows = pl.ds(pl.multiple_of(lax.rem(q, 2) * QW, TILE), QW)
            act_t[HALVES * f + q // 2, rows, c * TOK : (c + 1) * TOK] = act[c, f, :, q].reshape(TOK, QW).T
            return 0

        lax.fori_loop(0, SIDE, turned, 0)
        if (c, f) == (CHUNKS - 1, HALVES - 1):
            lax.fori_loop(0, SIDE, weight_grads, 0)

    def weight_grads(b, _):
        tokens = CHUNKS * TOK
        f, h = b // 2, lax.rem(b, 2)
        grads = beside([grad[:, f, 2 * h + k].reshape(tokens, QW) for k in range(2)])
        wide = dot(xt[...], grads, 0)
        for i in range(SUB):
            for j in range(SUB):
                rows, cols = slice(i * TILE, (i + 1) * TILE), slice(j * TILE, (j + 1) * TILE)
                up[b, rows, cols] = (wide[rows, cols] * mask_up[i, b * SUB + j].astype(F32)).astype(BF16)
        wide = dot(act_t[b], xin[:, :, 1].reshape(tokens, FEAT), 0)
        for i in range(SUB):
            for j in range(SUB):
                rows, cols = slice(i * TILE, (i + 1) * TILE), slice(j * TILE, (j + 1) * TILE)
                down[b, rows, cols] = (wide[rows, cols] * mask_down[j, b * SUB + i].astype(F32)).astype(BF16)
        return 0

    def finish(c, _):
        await_bytes(r9.at[c], recv_col.at[c, 2])
        for k, out in enumerate((outputs, grad_inputs)):
            total = po[c, col, k].astype(F32)
            for j in range(COLS - 1):
                total += r9[c, j, k].astype(F32)
            out[c] = total.astype(BF16)

    stages = (
        multiply_in, add_first, add_second, add_third, activate,
        spread_first, spread_second, spread_third, multiply_out, finish,
    )
    for stage, part in ORDER:
        stages[stage](part // HALVES, part % HALVES)
    half, quarter, eighth = ph.at[pl.ds(0, 2)], ph.at[0], ph.at[0, 0]
    sent = {Z0: xin.at[:, pl.ds(0, 3)], K0: xin.at[:, pl.ds(0, 4)], S1: half, S2: ph, S3: eighth, S4: quarter}
    sent.update({S5: quarter, S6: eighth, S7: ph, S8: half, S9: r9})
    for step, like in sent.items():
        await_bytes(like, send.at[step])


def run_block(inputs, w_up, w_down, mask_up, mask_down, cotangent):
    vmem = pl.BlockSpec(memory_space=pltpu.VMEM)
    hbm = pl.BlockSpec(memory_space=pl.ANY)

    def buf(*dims):
        return pltpu.VMEM((CHUNKS, *dims), BF16)

    def part(*dims):
        return buf(HALVES, *dims, BLK, QW)

    return pl.pallas_call(
        block_kernel,
        out_shape=[
            buf(ROWS, FEAT),
            buf(ROWS, FEAT),
            pltpu.VMEM((SIDE, FEAT, FEAT), BF16),
            pltpu.VMEM((SIDE, FEAT, FEAT), BF16),
        ],
        in_specs=[hbm] * 6,
        out_specs=[vmem] * 4,
        scratch_shapes=[
            buf(COLS, 2, ROWS, FEAT),
            pltpu.VMEM((FEAT, CHUNKS * TOK), BF16),
            pltpu.VMEM((SIDE, FEAT, CHUNKS * TOK), BF16),
            part(SIDE, SIDE),
            part(SIDE, SIDE),
            part(SIDE, SIDE),
            part(2, 2),
            part(2, 2),
            part(2, SIDE),
            part(2, SIDE),
            part(SIDE),
            part(SIDE),
            buf(HALVES, 2, ROWS, QW),
            buf(HALVES, 2, ROWS, QW),
            part(2),
            part(2),
            part(SIDE, SIDE),
            pltpu.VMEM((CHUNKS, 2, TOK, FEAT), F32),
            buf(COLS, 2, ROWS, FEAT),
            buf(COLS - 1, 2, ROWS, FEAT),
            pltpu.SMEM((SUB, SIDE * SUB), jnp.int32),
            pltpu.SMEM((SUB, SIDE * SUB), jnp.int32),
            pltpu.SemaphoreType.DMA((11,)),
            pltpu.SemaphoreType.DMA((CHUNKS, HALVES, 8)),
            pltpu.SemaphoreType.DMA((CHUNKS, 3)),
            pltpu.SemaphoreType.DMA((2, SIDE)),
            pltpu.SemaphoreType.DMA((4,)),
        ],
        compiler_params=pltpu.CompilerParams(
            collective_id=0, has_side_effects=True, vmem_limit_bytes=48 * 2**20
        ),
    )(
        inputs.reshape(CHUNKS, ROWS, FEAT),
        w_up,
        w_down,
        mask_up,
        mask_down.T,
        cotangent.reshape(CHUNKS, ROWS, FEAT),
    )


def store_kernel(out_here, gin_here, up, down, outputs, grad_inputs, gup, gdown, sems):
    moves = []
    for b in range(SIDE):
        units = pl.ds(b * FEAT, FEAT)
        moves.append(pltpu.make_async_copy(up.at[b], gup.at[:, units], sems.at[2 * b]))
        moves.append(pltpu.make_async_copy(down.at[b], gdown.at[units], sems.at[2 * b + 1]))
    moves.append(pltpu.make_async_copy(out_here, outputs, sems.at[2 * SIDE]))
    moves.append(pltpu.make_async_copy(gin_here, grad_inputs, sems.at[2 * SIDE + 1]))
    for copy in moves:
        copy.start()
    for copy in moves:
        copy.wait()


def store(outputs, grad_inputs, up, down):
    vmem = pl.BlockSpec(memory_space=pltpu.VMEM)
    hbm = pl.BlockSpec(memory_space=pl.ANY)
    return pl.pallas_call(
        store_kernel,
        out_shape=[
            jax.ShapeDtypeStruct(outputs.shape, BF16),
            jax.ShapeDtypeStruct(outputs.shape, BF16),
            jax.ShapeDtypeStruct((FEAT, SIDE * FEAT), BF16),
            jax.ShapeDtypeStruct((SIDE * FEAT, FEAT), BF16),
        ],
        in_specs=[vmem] * 4,
        out_specs=[hbm] * 4,
        scratch_shapes=[pltpu.SemaphoreType.DMA((2 * SIDE + 2,))],
        compiler_params=pltpu.CompilerParams(vmem_limit_bytes=8 * 2**20),
    )(outputs, grad_inputs, up, down)


def per_device(inputs, w_up, w_down, mask_up, mask_down, cotangent):
    kept = run_block(inputs, w_up, w_down, mask_up, mask_down, cotangent)
    outputs, grad_inputs, grad_up, grad_down = store(
        *(pltpu.with_memory_space_constraint(array, pltpu.VMEM) for array in kept)
    )
    return (outputs.reshape(inputs.shape), grad_inputs.reshape(inputs.shape), grad_up, grad_down)


def solution(mesh):
    in_specs = (
        P("col", "row"),
        P("row", "col"),
        P("col", "row"),
        P("row", "col"),
        P("col", "row"),
        P("col", "row"),
    )
    out_specs = (P("col", "row"), P("col", "row"), P("row", "col"), P("col", "row"))
    return jax.shard_map(
        per_device, mesh=mesh, in_specs=in_specs, out_specs=out_specs, check_vma=False
    )
```

```python
import functools

import jax
import jax.numpy as jnp
from jax import lax
from jax.experimental import pallas as pl
from jax.experimental.pallas import tpu as pltpu
from jax.sharding import PartitionSpec as P

MESH = pl.DeviceIdType.MESH
BF16 = jnp.bfloat16
F32 = jnp.float32
SIDE = 4
CHUNKS = 4
HALVES = 2
COLS = 8
ROWS = 16
TOK = COLS * ROWS
BLK = TOK // SIDE
FEAT = 768
QW = 384
TILE = 128
SUB = FEAT // TILE
Z0, K0, S1, S2, S3, S4, S5, S6, S7, S8, K9, Z9 = range(12)

ORDER = (
    (9, 0), (0, 0), (9, 1), (0, 1), (9, 2), (0, 2), (9, 3), (1, 0), (0, 3), (1, 1), (0, 4), (1, 2), (0, 5), (2, 0),
    (1, 3), (0, 6), (2, 1), (1, 4), (0, 7), (2, 2), (1, 5), (3, 0), (2, 3), (1, 6), (3, 1), (2, 4), (1, 7), (3, 2),
    (2, 5), (4, 0), (3, 3), (2, 6), (4, 1), (3, 4), (2, 7), (4, 2), (3, 5), (5, 0), (4, 3), (3, 6), (5, 1), (4, 4),
    (3, 7), (5, 2), (4, 5), (6, 0), (5, 3), (4, 6), (6, 1), (5, 4), (4, 7), (6, 2), (5, 5), (7, 0), (6, 3), (5, 6),
    (7, 1), (6, 4), (5, 7), (7, 2), (6, 5), (8, 0), (7, 3), (6, 6), (8, 1), (7, 4), (6, 7), (10, 0), (8, 2), (7, 5),
    (8, 3), (11, 0), (7, 6), (10, 1), (8, 4), (7, 7), (8, 5), (8, 6), (11, 1), (10, 2), (8, 7), (12, 0), (10, 3),
    (12, 1), (11, 2), (12, 2), (12, 3), (11, 3),
)


def beside(parts):
    return jnp.concatenate(parts, axis=1)


def dot(left, right, right_dim):
    return lax.dot_general(left, right, (((1,), (right_dim,)), ((), ())), preferred_element_type=F32)


def block_kernel(
    inputs, w_up, w_down, up_bits, down_bits, cotangent,
    outputs, grad_inputs, up, down,
    xin, xt, act_t, grad, ph, pg, r1h, r1g, r2h, r2g, sh, sg, r3h, r3g, r4h, r4g, act, acc, po, rk, r9, mask_up, mask_down,
    send, recv, recv_col, wsem, lsem,
):
    row, col = lax.axis_index("row"), lax.axis_index("col")
    x, y = row // SIDE, lax.rem(row, SIDE)
    z, core = col // 2, lax.rem(col, 2)

    def turn(v, by):
        return lax.rem(v + by, SIDE)

    def at_x(by):
        return (turn(x, by) * SIDE + y, col)

    def at_y(by):
        return (x * SIDE + turn(y, by), col)

    def at_z(by):
        return (row, 2 * turn(z, by) + core)

    barrier = pltpu.get_barrier_semaphore()
    sibling = (row, 2 * z + 1 - core)
    partners = [at_z(j) for j in (1, 2, 3)] + [sibling, at_x(1), at_x(3), at_y(1), at_y(3)]
    for device in partners:
        pl.semaphore_signal(barrier, inc=1, device_id=device, device_id_type=MESH)

    own = [
        pltpu.make_async_copy(up_bits, mask_up, lsem.at[2]),
        pltpu.make_async_copy(down_bits, mask_down, lsem.at[3]),
        pltpu.make_async_copy(inputs, xin.at[:, col, 0], lsem.at[0]),
        pltpu.make_async_copy(cotangent, xin.at[:, col, 1], lsem.at[1]),
    ]
    for copy in own:
        copy.start()
    loads = []
    for b in range(SIDE):
        units = pl.ds(b * FEAT, FEAT)
        loads.append(
            (
                pltpu.make_async_copy(w_up.at[:, units], up.at[b], wsem.at[0, b]),
                pltpu.make_async_copy(w_down.at[units], down.at[b], wsem.at[1, b]),
            )
        )
    for pair in loads:
        for copy in pair:
            copy.start()
    for copy in own:
        copy.wait()
    pl.semaphore_wait(barrier, len(partners))

    def ship(step, landed, src, dst, device):
        pltpu.make_async_remote_copy(
            src_ref=src,
            dst_ref=dst,
            send_sem=send.at[step],
            recv_sem=landed,
            device_id=device,
            device_id_type=MESH,
        ).start()

    def await_bytes(like, sem):
        pltpu.make_async_copy(like, like, sem).wait()

    def land(c, f, step):
        like = {S1: ph.at[c, f, pl.ds(0, 2)], S2: ph.at[c, f], S3: ph.at[c, f, 0, pl.ds(0, 2)], S4: ph.at[c, f, 0]}
        like.update({S5: like[S4], S6: like[S3], S7: like[S2], S8: like[S1]})
        await_bytes(like[step], recv.at[c, f, step - S1])

    def gather_z(c):
        for j in (1, 2, 3):
            ship(Z0, recv_col.at[c, 0], xin.at[c, col], xin.at[c, col], at_z(j))
        ship(K0, recv_col.at[c, 1], xin.at[c, col], xin.at[c, col], sibling)

    def gather_core(c):
        await_bytes(xin.at[c, pl.ds(0, 3)], recv_col.at[c, 0])
        for j in (1, 2, 3):
            there = 2 * turn(z, j) + core
            ship(K0, recv_col.at[c, 1], xin.at[c, there], xin.at[c, there], sibling)
        if c == 0:
            gather_z(3)

    gather_z(0)

    def drop_tiles(q, _):
        def one_row(i, _):
            rows = pl.ds(pl.multiple_of(i * TILE, TILE), TILE)
            for j in range(SUB):
                cols = pl.ds(j * TILE, TILE)
                up[q, rows, cols] = up[q, rows, cols] * mask_up[i, q * SUB + j].astype(F32).astype(BF16)
                down[q, rows, cols] = down[q, rows, cols] * mask_down[j, q * SUB + i].astype(F32).astype(BF16)
            return 0

        return lax.fori_loop(0, SUB, one_row, 0)

    for b in range(SIDE):
        for copy in loads[b]:
            copy.wait()
        drop_tiles(b, 0)
        if b == 1:
            gather_z(1)
    gather_z(2)

    def multiply_in(c, f):
        if f == 0:
            await_bytes(xin.at[c, pl.ds(0, SIDE)], recv_col.at[c, 1])

        def ahead(n, _):
            ins = xin[c, :, 0].reshape(TOK, FEAT)
            wide = dot(ins, up[HALVES * f + n], 0).astype(BF16)
            for k in range(2):
                ph[c, f, :, 2 * n + k] = wide[:, k * QW : (k + 1) * QW].reshape(SIDE, BLK, QW)
            return 0

        def back(k, _):
            n = lax.rem(y // 2 + k, 2)
            cot = xin[c, :, 1].reshape(TOK, FEAT)
            wide = dot(cot, down[HALVES * f + n], 1).astype(BF16)
            for k in range(2):
                pg[c, f, 2 * n + k] = wide[:, k * QW : (k + 1) * QW].reshape(SIDE, BLK, QW)
            return 0

        landed = recv.at[c, f, 0]
        low, high = pl.ds(0, 2), pl.ds(2, 2)
        lax.fori_loop(1, 2, back, 0)
        ship(S1, landed, pg.at[c, f, turn(y, 2), low], r1g.at[c, f, 0], at_y(1))
        ship(S1, landed, pg.at[c, f, turn(y, 2), high], r1g.at[c, f, 1], at_y(3))
        lax.fori_loop(0, 1, ahead, 0)
        ship(S1, landed, ph.at[c, f, turn(x, 2), low], r1h.at[c, f, 0], at_x(1))
        lax.fori_loop(1, 2, ahead, 0)
        ship(S1, landed, ph.at[c, f, turn(x, 2), high], r1h.at[c, f, 1], at_x(3))
        lax.fori_loop(2, 3, back, 0)

    def add_first(c, f):
        land(c, f, S1)

        def half(k, _):
            ph[c, f, turn(x, 1), k] += r1h[c, f, 0, k]
            pg[c, f, turn(y, 1), k] += r1g[c, f, 0, k]
            ph[c, f, turn(x, 3), 2 + k] += r1h[c, f, 1, k]
            pg[c, f, turn(y, 3), 2 + k] += r1g[c, f, 1, k]
            return 0

        lax.fori_loop(0, 2, half, 0)
        landed = recv.at[c, f, S2 - S1]
        ship(S2, landed, ph.at[c, f, turn(x, 1)], r2h.at[c, f, 0], at_x(1))
        ship(S2, landed, pg.at[c, f, turn(y, 1)], r2g.at[c, f, 0], at_y(1))
        ship(S2, landed, ph.at[c, f, turn(x, 3)], r2h.at[c, f, 1], at_x(3))
        ship(S2, landed, pg.at[c, f, turn(y, 3)], r2g.at[c, f, 1], at_y(3))

    def add_second(c, f):
        land(c, f, S2)

        def quarter(k, _):
            for own_part, come, total, at in ((ph, r2h, sh, x), (pg, r2g, sg, y)):
                total[c, f, k] = (
                    own_part[c, f, at, k].astype(F32) + come[c, f, 0, k].astype(F32) + come[c, f, 1, k].astype(F32)
                ).astype(BF16)
            return 0

        lax.fori_loop(0, SIDE, quarter, 0)
        landed = recv.at[c, f, S3 - S1]
        low, high = pl.ds(0, ROWS), pl.ds(ROWS, ROWS)
        ship(S3, landed, sh.at[c, f, turn(y, 2), low], r3h.at[c, f, 0], at_y(1))
        ship(S3, landed, sg.at[c, f, turn(x, 2), low], r3g.at[c, f, 0], at_x(1))
        ship(S3, landed, sh.at[c, f, turn(y, 2), high], r3h.at[c, f, 1], at_y(3))
        ship(S3, landed, sg.at[c, f, turn(x, 2), high], r3g.at[c, f, 1], at_x(3))

    def add_third(c, f):
        land(c, f, S3)
        low, high = pl.ds(0, ROWS), pl.ds(ROWS, ROWS)
        for total, come, at in ((sh, r3h, y), (sg, r3g, x)):
            total[c, f, turn(at, 1), low] += come[c, f, 0]
            total[c, f, turn(at, 3), high] += come[c, f, 1]
        landed = recv.at[c, f, S4 - S1]
        ship(S4, landed, sh.at[c, f, turn(y, 1)], r4h.at[c, f, 0], at_y(1))
        ship(S4, landed, sg.at[c, f, turn(x, 1)], r4g.at[c, f, 0], at_x(1))
        ship(S4, landed, sh.at[c, f, turn(y, 3)], r4h.at[c, f, 1], at_y(3))
        ship(S4, landed, sg.at[c, f, turn(x, 3)], r4g.at[c, f, 1], at_x(3))

    def activate(c, f):
        land(c, f, S4)

        def some_rows(i, _):
            rows = pl.ds(pl.multiple_of(i * ROWS, ROWS), ROWS)
            value, slope = sh[c, f, y, rows].astype(F32), sg[c, f, x, rows].astype(F32)
            for j in range(2):
                value += r4h[c, f, j, rows].astype(F32)
                slope += r4g[c, f, j, rows].astype(F32)
            root = 0.7978845608028654
            square = value * value
            tan = jnp.tanh(root * (value + 0.044715 * (square * value)))
            gate = 0.5 * (1.0 + tan)
            bend = 0.5 * value * (1.0 - tan * tan) * (root * (1.0 + 3.0 * 0.044715 * square))
            act[c, f, x, y, rows] = (value * gate).astype(BF16)
            grad[c, f, y, x, rows] = (slope * (gate + bend)).astype(BF16)
            return 0

        lax.fori_loop(0, BLK // ROWS, some_rows, 0)
        landed = recv.at[c, f, S5 - S1]
        for j in (1, 3):
            ship(S5, landed, act.at[c, f, x, y], act.at[c, f, x, y], at_y(j))
            ship(S5, landed, grad.at[c, f, y, x], grad.at[c, f, y, x], at_x(j))

    def spread_first(c, f):
        land(c, f, S5)
        low, high = pl.ds(0, ROWS), pl.ds(ROWS, ROWS)
        landed = recv.at[c, f, S6 - S1]
        left, right, under, over = turn(x, 3), turn(x, 1), turn(y, 3), turn(y, 1)
        ship(S6, landed, act.at[c, f, x, under, low], act.at[c, f, x, under, low], at_y(1))
        ship(S6, landed, grad.at[c, f, y, left, low], grad.at[c, f, y, left, low], at_x(1))
        ship(S6, landed, act.at[c, f, x, over, high], act.at[c, f, x, over, high], at_y(3))
        ship(S6, landed, grad.at[c, f, y, right, high], grad.at[c, f, y, right, high], at_x(3))
        if f == 0:
            xt[:, c * TOK : (c + 1) * TOK] = xin[c, :, 0].reshape(TOK, FEAT).T

    def spread_second(c, f):
        land(c, f, S6)
        landed = recv.at[c, f, S7 - S1]
        for j in (1, 3):
            ship(S7, landed, act.at[c, f, x], act.at[c, f, x], at_x(j))
            ship(S7, landed, grad.at[c, f, y], grad.at[c, f, y], at_y(j))

    def spread_third(c, f):
        land(c, f, S7)
        low, high = pl.ds(0, 2), pl.ds(2, 2)
        landed = recv.at[c, f, S8 - S1]
        left, right, under, over = turn(x, 3), turn(x, 1), turn(y, 3), turn(y, 1)
        ship(S8, landed, act.at[c, f, left, low], act.at[c, f, left, low], at_x(1))
        ship(S8, landed, grad.at[c, f, under, low], grad.at[c, f, under, low], at_y(1))
        ship(S8, landed, act.at[c, f, right, high], act.at[c, f, right, high], at_x(3))
        ship(S8, landed, grad.at[c, f, over, high], grad.at[c, f, over, high], at_y(3))

    def multiply_out(c, f):
        land(c, f, S8)
        for k in range(2):
            out = acc[c, k] if f else jnp.zeros((TOK, FEAT), F32)
            for h in range(2):
                b, quarters = HALVES * f + h, (2 * h, 2 * h + 1)
                if k == 0:
                    left = beside([act[c, f, :, q].reshape(TOK, QW) for q in quarters])
                    out += dot(left, down[b], 0)
                else:
                    left = beside([grad[c, f, q].reshape(TOK, QW) for q in quarters])
                    out += dot(left, up[b], 1)
            if f == 0:
                acc[c, k] = out
            else:
                slabs = out.astype(BF16).reshape(SIDE, 2, ROWS, FEAT)
                for k2 in range(2):
                    po[c, k, k2] = slabs[:, k2]
                ship(K9, recv_col.at[c, 2 + k], po.at[c, k, 1 - core], rk.at[c, k], sibling)
        if c + 1 < CHUNKS:
            turn_act(c, f)

    def turn_act(c, f):
        def turned(q, _):
            rows = pl.ds(pl.multiple_of(lax.rem(q, 2) * QW, TILE), QW)
            act_t[HALVES * f + q // 2, rows, c * TOK : (c + 1) * TOK] = act[c, f, :, q].reshape(TOK, QW).T
            return 0

        lax.fori_loop(0, SIDE, turned, 0)

    def weight_grads(b):
        tokens = CHUNKS * TOK
        f, h = b // 2, b % 2
        if h == 0:
            turn_act(CHUNKS - 1, f)
        grads = beside([grad[:, f, 2 * h + k].reshape(tokens, QW) for k in range(2)])
        wide = dot(xt[...], grads, 0)
        for i in range(SUB):
            for j in range(SUB):
                rows, cols = slice(i * TILE, (i + 1) * TILE), slice(j * TILE, (j + 1) * TILE)
                up[b, rows, cols] = (wide[rows, cols] * mask_up[i, b * SUB + j].astype(F32)).astype(BF16)
        wide = dot(act_t[b], xin[:, :, 1].reshape(tokens, FEAT), 0)
        for i in range(SUB):
            for j in range(SUB):
                rows, cols = slice(i * TILE, (i + 1) * TILE), slice(j * TILE, (j + 1) * TILE)
                down[b, rows, cols] = (wide[rows, cols] * mask_down[j, b * SUB + i].astype(F32)).astype(BF16)

    def sum_core(c):
        for k in range(2):
            await_bytes(rk.at[c, k], recv_col.at[c, 2 + k])
            po[c, k, core] = (po[c, k, core].astype(F32) + rk[c, k].astype(F32)).astype(BF16)
            for j in (1, 2, 3):
                ship(Z9, recv_col.at[c, 4], po.at[c, k, core, turn(z, j)], r9.at[c, j - 1, k], at_z(j))

    def finish(c):
        await_bytes(r9.at[c], recv_col.at[c, 4])
        for k, out in enumerate((outputs, grad_inputs)):
            total = po[c, k, core, z].astype(F32)
            for j in range(SIDE - 1):
                total += r9[c, j, k].astype(F32)
            out[c] = total.astype(BF16)

    stages = (
        multiply_in, add_first, add_second, add_third, activate, spread_first, spread_second, spread_third, multiply_out,
        gather_core, sum_core, finish, weight_grads,
    )
    for stage, n in ORDER:
        stages[stage](*((n // HALVES, n % HALVES) if stage < 9 else (n,)))
    half, quarter, eighth = ph.at[pl.ds(0, 2)], ph.at[0], ph.at[0, 0]
    sent = {Z0: xin.at[:, pl.ds(0, 3)], K0: xin.at[:, pl.ds(0, 4)], S1: half, S2: ph, S3: eighth, S4: quarter}
    sent.update({S5: quarter, S6: eighth, S7: ph, S8: half, K9: po.at[pl.ds(0, 2)], Z9: r9})
    for step, like in sent.items():
        await_bytes(like, send.at[step])


def run_block(inputs, w_up, w_down, mask_up, mask_down, cotangent):
    vmem = pl.BlockSpec(memory_space=pltpu.VMEM)
    hbm = pl.BlockSpec(memory_space=pl.ANY)

    def buf(*dims):
        return pltpu.VMEM((CHUNKS, *dims), BF16)

    def part(*dims):
        return buf(HALVES, *dims, BLK, QW)

    return pl.pallas_call(
        block_kernel,
        out_shape=[
            buf(ROWS, FEAT),
            buf(ROWS, FEAT),
            pltpu.VMEM((SIDE, FEAT, FEAT), BF16),
            pltpu.VMEM((SIDE, FEAT, FEAT), BF16),
        ],
        in_specs=[hbm] * 6,
        out_specs=[vmem] * 4,
        scratch_shapes=[
            buf(COLS, 2, ROWS, FEAT),
            pltpu.VMEM((FEAT, CHUNKS * TOK), BF16),
            pltpu.VMEM((SIDE, FEAT, CHUNKS * TOK), BF16),
            part(SIDE, SIDE),
            part(SIDE, SIDE),
            part(SIDE, SIDE),
            part(2, 2),
            part(2, 2),
            part(2, SIDE),
            part(2, SIDE),
            part(SIDE),
            part(SIDE),
            buf(HALVES, 2, ROWS, QW),
            buf(HALVES, 2, ROWS, QW),
            part(2),
            part(2),
            part(SIDE, SIDE),
            pltpu.VMEM((CHUNKS, 2, TOK, FEAT), F32),
            buf(2, 2, SIDE, ROWS, FEAT),
            buf(2, SIDE, ROWS, FEAT),
            buf(SIDE - 1, 2, ROWS, FEAT),
            pltpu.SMEM((SUB, SIDE * SUB), jnp.int32),
            pltpu.SMEM((SUB, SIDE * SUB), jnp.int32),
            pltpu.SemaphoreType.DMA((12,)),
            pltpu.SemaphoreType.DMA((CHUNKS, HALVES, 8)),
            pltpu.SemaphoreType.DMA((CHUNKS, 5)),
            pltpu.SemaphoreType.DMA((2, SIDE)),
            pltpu.SemaphoreType.DMA((4,)),
        ],
        compiler_params=pltpu.CompilerParams(
            collective_id=0, has_side_effects=True, vmem_limit_bytes=48 * 2**20
        ),
    )(
        inputs.reshape(CHUNKS, ROWS, FEAT),
        w_up,
        w_down,
        mask_up,
        mask_down.T,
        cotangent.reshape(CHUNKS, ROWS, FEAT),
    )


def store_kernel(out_here, gin_here, up, down, outputs, grad_inputs, gup, gdown, sems):
    moves = []
    for b in range(SIDE):
        units = pl.ds(b * FEAT, FEAT)
        moves.append(pltpu.make_async_copy(up.at[b], gup.at[:, units], sems.at[2 * b]))
        moves.append(pltpu.make_async_copy(down.at[b], gdown.at[units], sems.at[2 * b + 1]))
    moves.append(pltpu.make_async_copy(out_here, outputs, sems.at[2 * SIDE]))
    moves.append(pltpu.make_async_copy(gin_here, grad_inputs, sems.at[2 * SIDE + 1]))
    for copy in moves:
        copy.start()
    for copy in moves:
        copy.wait()


def store(outputs, grad_inputs, up, down):
    vmem = pl.BlockSpec(memory_space=pltpu.VMEM)
    hbm = pl.BlockSpec(memory_space=pl.ANY)
    return pl.pallas_call(
        store_kernel,
        out_shape=[
            jax.ShapeDtypeStruct(outputs.shape, BF16),
            jax.ShapeDtypeStruct(outputs.shape, BF16),
            jax.ShapeDtypeStruct((FEAT, SIDE * FEAT), BF16),
            jax.ShapeDtypeStruct((SIDE * FEAT, FEAT), BF16),
        ],
        in_specs=[vmem] * 4,
        out_specs=[hbm] * 4,
        scratch_shapes=[pltpu.SemaphoreType.DMA((2 * SIDE + 2,))],
        compiler_params=pltpu.CompilerParams(vmem_limit_bytes=8 * 2**20),
    )(outputs, grad_inputs, up, down)


def per_device(inputs, w_up, w_down, mask_up, mask_down, cotangent):
    kept = run_block(inputs, w_up, w_down, mask_up, mask_down, cotangent)
    outputs, grad_inputs, grad_up, grad_down = store(
        *(pltpu.with_memory_space_constraint(array, pltpu.VMEM) for array in kept)
    )
    return (outputs.reshape(inputs.shape), grad_inputs.reshape(inputs.shape), grad_up, grad_down)


def solution(mesh):
    in_specs = (
        P("col", "row"),
        P("row", "col"),
        P("col", "row"),
        P("row", "col"),
        P("col", "row"),
        P("col", "row"),
    )
    out_specs = (P("col", "row"), P("col", "row"), P("row", "col"), P("col", "row"))
    return jax.shard_map(
        per_device, mesh=mesh, in_specs=in_specs, out_specs=out_specs, check_vma=False
    )
```

```python
import functools

import jax
import jax.numpy as jnp
from jax import lax
from jax.experimental import pallas as pl
from jax.experimental.pallas import tpu as pltpu
from jax.sharding import PartitionSpec as P

MESH = pl.DeviceIdType.MESH
BF16 = jnp.bfloat16
F32 = jnp.float32
SIDE = 4
CHUNKS = 4
HALVES = 2
COLS = 8
ROWS = 16
TOK = COLS * ROWS
BLK = TOK // SIDE
FEAT = 768
QW = 384
TILE = 128
SUB = FEAT // TILE
Z0, K0, S1, S2, S3, S4, S5, S6, S7, S8, K9, Z9 = range(12)

ORDER = (
    (9, 0), (0, 0), (9, 1), (0, 1), (9, 2), (0, 2), (9, 3), (1, 0), (0, 3), (1, 1), (0, 4), (1, 2), (0, 5), (2, 0),
    (1, 3), (0, 6), (2, 1), (1, 4), (0, 7), (2, 2), (1, 5), (3, 0), (2, 3), (1, 6), (3, 1), (2, 4), (1, 7), (3, 2),
    (2, 5), (4, 0), (3, 3), (2, 6), (4, 1), (3, 4), (2, 7), (4, 2), (3, 5), (5, 0), (4, 3), (3, 6), (5, 1), (4, 4),
    (3, 7), (5, 2), (4, 5), (6, 0), (5, 3), (4, 6), (6, 1), (5, 4), (4, 7), (6, 2), (5, 5), (7, 0), (6, 3), (5, 6),
    (7, 1), (6, 4), (5, 7), (7, 2), (6, 5), (8, 0), (7, 3), (6, 6), (8, 1), (7, 4), (6, 7), (10, 0), (8, 2), (7, 5),
    (8, 3), (11, 0), (7, 6), (10, 1), (8, 4), (7, 7), (8, 5), (8, 6), (11, 1), (10, 2), (8, 7), (12, 0), (10, 3),
    (12, 1), (11, 2), (12, 2), (12, 3), (11, 3),
)


def beside(parts):
    return jnp.concatenate(parts, axis=1)


def dot(left, right, right_dim):
    return lax.dot_general(left, right, (((1,), (right_dim,)), ((), ())), preferred_element_type=F32)


def block_kernel(
    inputs, w_up, w_down, up_bits, down_bits, cotangent,
    outputs, grad_inputs, up, down,
    xin, xt, act_t, grad, ph, pg, r1h, r1g, r2h, r2g, sh, sg, r3h, r3g, r4h, r4g, act, acc, po, rk, r9, mask_up, mask_down,
    send, recv, recv_col, wsem, lsem,
):
    row, col = lax.axis_index("row"), lax.axis_index("col")
    x, y = row // SIDE, lax.rem(row, SIDE)
    z, core = col // 2, lax.rem(col, 2)

    def turn(v, by):
        return lax.rem(v + by, SIDE)

    def at_x(by):
        return (turn(x, by) * SIDE + y, col)

    def at_y(by):
        return (x * SIDE + turn(y, by), col)

    def at_z(by):
        return (row, 2 * turn(z, by) + core)

    barrier = pltpu.get_barrier_semaphore()
    sibling = (row, 2 * z + 1 - core)
    partners = [at_z(j) for j in (1, 2, 3)] + [sibling, at_x(1), at_x(3), at_y(1), at_y(3)]
    for device in partners:
        pl.semaphore_signal(barrier, inc=1, device_id=device, device_id_type=MESH)

    own = [
        pltpu.make_async_copy(up_bits, mask_up, lsem.at[2]),
        pltpu.make_async_copy(down_bits, mask_down, lsem.at[3]),
        pltpu.make_async_copy(inputs, xin.at[:, col, 0], lsem.at[0]),
        pltpu.make_async_copy(cotangent, xin.at[:, col, 1], lsem.at[1]),
    ]
    for copy in own:
        copy.start()
    loads = []
    for b in range(SIDE):
        units = pl.ds(b * FEAT, FEAT)
        loads.append(
            (
                pltpu.make_async_copy(w_up.at[:, units], up.at[b], wsem.at[0, b]),
                pltpu.make_async_copy(w_down.at[units], down.at[b], wsem.at[1, b]),
            )
        )
    for pair in loads:
        for copy in pair:
            copy.start()
    for copy in own:
        copy.wait()
    pl.semaphore_wait(barrier, len(partners))

    def ship(step, landed, src, dst, device):
        pltpu.make_async_remote_copy(
            src_ref=src,
            dst_ref=dst,
            send_sem=send.at[step],
            recv_sem=landed,
            device_id=device,
            device_id_type=MESH,
        ).start()

    def await_bytes(like, sem):
        pltpu.make_async_copy(like, like, sem).wait()

    def land(c, f, step):
        like = {S1: ph.at[c, f, pl.ds(0, 2)], S2: ph.at[c, f], S3: ph.at[c, f, 0, pl.ds(0, 2)], S4: ph.at[c, f, 0]}
        like.update({S5: like[S4], S6: like[S3], S7: like[S2], S8: like[S1]})
        await_bytes(like[step], recv.at[c, f, step - S1])

    def gather_z(c):
        for j in (1, 2, 3):
            ship(Z0, recv_col.at[c, 0], xin.at[c, col], xin.at[c, col], at_z(j))
        ship(K0, recv_col.at[c, 1], xin.at[c, col], xin.at[c, col], sibling)

    def gather_core(c):
        await_bytes(xin.at[c, pl.ds(0, 3)], recv_col.at[c, 0])
        for j in (1, 2, 3):
            there = 2 * turn(z, j) + core
            ship(K0, recv_col.at[c, 1], xin.at[c, there], xin.at[c, there], sibling)
        if c == 0:
            gather_z(3)

    gather_z(0)

    def drop_tiles(q, _):
        def one_row(i, _):
            rows = pl.ds(pl.multiple_of(i * TILE, TILE), TILE)
            for j in range(SUB):
                cols = pl.ds(j * TILE, TILE)
                up[q, rows, cols] = up[q, rows, cols] * mask_up[i, q * SUB + j].astype(F32).astype(BF16)
                down[q, rows, cols] = down[q, rows, cols] * mask_down[j, q * SUB + i].astype(F32).astype(BF16)
            return 0

        return lax.fori_loop(0, SUB, one_row, 0)

    for b in range(SIDE):
        for copy in loads[b]:
            copy.wait()
        drop_tiles(b, 0)
        if b == 1:
            gather_z(1)
    gather_z(2)

    def multiply_in(c, f):
        if f == 0:
            await_bytes(xin.at[c, pl.ds(0, SIDE)], recv_col.at[c, 1])

        def ahead(n, _):
            ins = xin[c, :, 0].reshape(TOK, FEAT)
            wide = dot(ins, up[HALVES * f + n], 0).astype(BF16)
            for k in range(2):
                ph[c, f, :, 2 * n + k] = wide[:, k * QW : (k + 1) * QW].reshape(SIDE, BLK, QW)
            return 0

        def back(k, _):
            n = lax.rem(y // 2 + k, 2)
            cot = xin[c, :, 1].reshape(TOK, FEAT)
            wide = dot(cot, down[HALVES * f + n], 1).astype(BF16)
            for k in range(2):
                pg[c, f, 2 * n + k] = wide[:, k * QW : (k + 1) * QW].reshape(SIDE, BLK, QW)
            return 0

        landed = recv.at[c, f, 0]
        low, high = pl.ds(0, 2), pl.ds(2, 2)
        lax.fori_loop(1, 2, back, 0)
        ship(S1, landed, pg.at[c, f, turn(y, 2), low], r1g.at[c, f, 0], at_y(1))
        ship(S1, landed, pg.at[c, f, turn(y, 2), high], r1g.at[c, f, 1], at_y(3))
        lax.fori_loop(0, 1, ahead, 0)
        ship(S1, landed, ph.at[c, f, turn(x, 2), low], r1h.at[c, f, 0], at_x(1))
        lax.fori_loop(1, 2, ahead, 0)
        ship(S1, landed, ph.at[c, f, turn(x, 2), high], r1h.at[c, f, 1], at_x(3))
        lax.fori_loop(2, 3, back, 0)

    def add_first(c, f):
        land(c, f, S1)

        def half(k, _):
            ph[c, f, turn(x, 1), k] += r1h[c, f, 0, k]
            pg[c, f, turn(y, 1), k] += r1g[c, f, 0, k]
            ph[c, f, turn(x, 3), 2 + k] += r1h[c, f, 1, k]
            pg[c, f, turn(y, 3), 2 + k] += r1g[c, f, 1, k]
            return 0

        lax.fori_loop(0, 2, half, 0)
        landed = recv.at[c, f, S2 - S1]
        ship(S2, landed, ph.at[c, f, turn(x, 1)], r2h.at[c, f, 0], at_x(1))
        ship(S2, landed, pg.at[c, f, turn(y, 1)], r2g.at[c, f, 0], at_y(1))
        ship(S2, landed, ph.at[c, f, turn(x, 3)], r2h.at[c, f, 1], at_x(3))
        ship(S2, landed, pg.at[c, f, turn(y, 3)], r2g.at[c, f, 1], at_y(3))

    def add_second(c, f):
        land(c, f, S2)

        def quarter(k, _):
            for own_part, come, total, at in ((ph, r2h, sh, x), (pg, r2g, sg, y)):
                total[c, f, k] = (
                    own_part[c, f, at, k].astype(F32) + come[c, f, 0, k].astype(F32) + come[c, f, 1, k].astype(F32)
                ).astype(BF16)
            return 0

        lax.fori_loop(0, SIDE, quarter, 0)
        landed = recv.at[c, f, S3 - S1]
        low, high = pl.ds(0, ROWS), pl.ds(ROWS, ROWS)
        ship(S3, landed, sh.at[c, f, turn(y, 2), low], r3h.at[c, f, 0], at_y(1))
        ship(S3, landed, sg.at[c, f, turn(x, 2), low], r3g.at[c, f, 0], at_x(1))
        ship(S3, landed, sh.at[c, f, turn(y, 2), high], r3h.at[c, f, 1], at_y(3))
        ship(S3, landed, sg.at[c, f, turn(x, 2), high], r3g.at[c, f, 1], at_x(3))

    def add_third(c, f):
        land(c, f, S3)
        low, high = pl.ds(0, ROWS), pl.ds(ROWS, ROWS)
        for total, come, at in ((sh, r3h, y), (sg, r3g, x)):
            total[c, f, turn(at, 1), low] += come[c, f, 0]
            total[c, f, turn(at, 3), high] += come[c, f, 1]
        landed = recv.at[c, f, S4 - S1]
        ship(S4, landed, sh.at[c, f, turn(y, 1)], r4h.at[c, f, 0], at_y(1))
        ship(S4, landed, sg.at[c, f, turn(x, 1)], r4g.at[c, f, 0], at_x(1))
        ship(S4, landed, sh.at[c, f, turn(y, 3)], r4h.at[c, f, 1], at_y(3))
        ship(S4, landed, sg.at[c, f, turn(x, 3)], r4g.at[c, f, 1], at_x(3))

    def activate(c, f):
        land(c, f, S4)

        def some_rows(i, _):
            rows = pl.ds(pl.multiple_of(i * ROWS, ROWS), ROWS)
            value, slope = sh[c, f, y, rows].astype(F32), sg[c, f, x, rows].astype(F32)
            for j in range(2):
                value += r4h[c, f, j, rows].astype(F32)
                slope += r4g[c, f, j, rows].astype(F32)
            root = 0.7978845608028654
            square = value * value
            tan = jnp.tanh(root * (value + 0.044715 * (square * value)))
            gate = 0.5 * (1.0 + tan)
            bend = 0.5 * value * (1.0 - tan * tan) * (root * (1.0 + 3.0 * 0.044715 * square))
            act[c, f, x, y, rows] = (value * gate).astype(BF16)
            grad[c, f, y, x, rows] = (slope * (gate + bend)).astype(BF16)
            return 0

        lax.fori_loop(0, BLK // ROWS, some_rows, 0)
        landed = recv.at[c, f, S5 - S1]
        for j in (1, 3):
            ship(S5, landed, act.at[c, f, x, y], act.at[c, f, x, y], at_y(j))
            ship(S5, landed, grad.at[c, f, y, x], grad.at[c, f, y, x], at_x(j))

    def spread_first(c, f):
        land(c, f, S5)
        low, high = pl.ds(0, ROWS), pl.ds(ROWS, ROWS)
        landed = recv.at[c, f, S6 - S1]
        left, right, under, over = turn(x, 3), turn(x, 1), turn(y, 3), turn(y, 1)
        ship(S6, landed, act.at[c, f, x, under, low], act.at[c, f, x, under, low], at_y(1))
        ship(S6, landed, grad.at[c, f, y, left, low], grad.at[c, f, y, left, low], at_x(1))
        ship(S6, landed, act.at[c, f, x, over, high], act.at[c, f, x, over, high], at_y(3))
        ship(S6, landed, grad.at[c, f, y, right, high], grad.at[c, f, y, right, high], at_x(3))
        if f == 0:
            xt[:, c * TOK : (c + 1) * TOK] = xin[c, :, 0].reshape(TOK, FEAT).T

    def spread_second(c, f):
        land(c, f, S6)
        landed = recv.at[c, f, S7 - S1]
        for j in (1, 3):
            ship(S7, landed, act.at[c, f, x], act.at[c, f, x], at_x(j))
            ship(S7, landed, grad.at[c, f, y], grad.at[c, f, y], at_y(j))

    def spread_third(c, f):
        land(c, f, S7)
        low, high = pl.ds(0, 2), pl.ds(2, 2)
        landed = recv.at[c, f, S8 - S1]
        left, right, under, over = turn(x, 3), turn(x, 1), turn(y, 3), turn(y, 1)
        ship(S8, landed, act.at[c, f, left, low], act.at[c, f, left, low], at_x(1))
        ship(S8, landed, grad.at[c, f, under, low], grad.at[c, f, under, low], at_y(1))
        ship(S8, landed, act.at[c, f, right, high], act.at[c, f, right, high], at_x(3))
        ship(S8, landed, grad.at[c, f, over, high], grad.at[c, f, over, high], at_y(3))

    def multiply_out(c, f):
        land(c, f, S8)
        for k in range(2):
            out = acc[c, k] if f else jnp.zeros((TOK, FEAT), F32)
            for h in range(2):
                b, quarters = HALVES * f + h, (2 * h, 2 * h + 1)
                if k == 0:
                    left = beside([act[c, f, :, q].reshape(TOK, QW) for q in quarters])
                    out += dot(left, down[b], 0)
                else:
                    left = beside([grad[c, f, q].reshape(TOK, QW) for q in quarters])
                    out += dot(left, up[b], 1)
            if f == 0:
                acc[c, k] = out
            else:
                slabs = out.astype(BF16).reshape(SIDE, 2, ROWS, FEAT)
                for k2 in range(2):
                    po[c, k, k2] = slabs[:, k2]
                ship(K9, recv_col.at[c, 2 + k], po.at[c, k, 1 - core], rk.at[c, k], sibling)
        if c + 1 < CHUNKS:
            turn_act(c, f)

    def turn_act(c, f):
        def turned(q, _):
            rows = pl.ds(pl.multiple_of(lax.rem(q, 2) * QW, TILE), QW)
            act_t[HALVES * f + q // 2, rows, c * TOK : (c + 1) * TOK] = act[c, f, :, q].reshape(TOK, QW).T
            return 0

        lax.fori_loop(0, SIDE, turned, 0)

    def weight_grads(b):
        tokens = CHUNKS * TOK
        f, h = b // 2, b % 2
        if h == 0:
            turn_act(CHUNKS - 1, f)
        grads = beside([grad[:, f, 2 * h + k].reshape(tokens, QW) for k in range(2)])
        wide = dot(xt[...], grads, 0)
        for i in range(SUB):
            for j in range(SUB):
                rows, cols = slice(i * TILE, (i + 1) * TILE), slice(j * TILE, (j + 1) * TILE)
                up[b, rows, cols] = (wide[rows, cols] * mask_up[i, b * SUB + j].astype(F32)).astype(BF16)
        wide = dot(act_t[b], xin[:, :, 1].reshape(tokens, FEAT), 0)
        for i in range(SUB):
            for j in range(SUB):
                rows, cols = slice(i * TILE, (i + 1) * TILE), slice(j * TILE, (j + 1) * TILE)
                down[b, rows, cols] = (wide[rows, cols] * mask_down[j, b * SUB + i].astype(F32)).astype(BF16)

    def sum_core(c):
        for k in range(2):
            await_bytes(rk.at[c, k], recv_col.at[c, 2 + k])
            po[c, k, core] = (po[c, k, core].astype(F32) + rk[c, k].astype(F32)).astype(BF16)
            for j in (1, 2, 3):
                ship(Z9, recv_col.at[c, 4], po.at[c, k, core, turn(z, j)], r9.at[c, j - 1, k], at_z(j))

    def finish(c):
        await_bytes(r9.at[c], recv_col.at[c, 4])
        for k, out in enumerate((outputs, grad_inputs)):
            total = po[c, k, core, z].astype(F32)
            for j in range(SIDE - 1):
                total += r9[c, j, k].astype(F32)
            out[c] = total.astype(BF16)

    stages = (
        multiply_in, add_first, add_second, add_third, activate, spread_first, spread_second, spread_third, multiply_out,
        gather_core, sum_core, finish, weight_grads,
    )
    for stage, n in ORDER:
        stages[stage](*((n // HALVES, n % HALVES) if stage < 9 else (n,)))
    half, quarter, eighth = ph.at[pl.ds(0, 2)], ph.at[0], ph.at[0, 0]
    sent = {Z0: xin.at[:, pl.ds(0, 3)], K0: xin.at[:, pl.ds(0, 4)], S1: half, S2: ph, S3: eighth, S4: quarter}
    sent.update({S5: quarter, S6: eighth, S7: ph, S8: half, K9: po.at[pl.ds(0, 2)], Z9: r9})
    for step, like in sent.items():
        await_bytes(like, send.at[step])


def run_block(inputs, w_up, w_down, mask_up, mask_down, cotangent):
    vmem = pl.BlockSpec(memory_space=pltpu.VMEM)
    hbm = pl.BlockSpec(memory_space=pl.ANY)

    def buf(*dims):
        return pltpu.VMEM((CHUNKS, *dims), BF16)

    def part(*dims):
        return buf(HALVES, *dims, BLK, QW)

    return pl.pallas_call(
        block_kernel,
        out_shape=[
            buf(ROWS, FEAT),
            buf(ROWS, FEAT),
            pltpu.VMEM((SIDE, FEAT, FEAT), BF16),
            pltpu.VMEM((SIDE, FEAT, FEAT), BF16),
        ],
        in_specs=[hbm] * 6,
        out_specs=[vmem] * 4,
        scratch_shapes=[
            buf(COLS, 2, ROWS, FEAT),
            pltpu.VMEM((FEAT, CHUNKS * TOK), BF16),
            pltpu.VMEM((SIDE, FEAT, CHUNKS * TOK), BF16),
            part(SIDE, SIDE),
            part(SIDE, SIDE),
            part(SIDE, SIDE),
            part(2, 2),
            part(2, 2),
            part(2, SIDE),
            part(2, SIDE),
            part(SIDE),
            part(SIDE),
            buf(HALVES, 2, ROWS, QW),
            buf(HALVES, 2, ROWS, QW),
            part(2),
            part(2),
            part(SIDE, SIDE),
            pltpu.VMEM((CHUNKS, 2, TOK, FEAT), F32),
            buf(2, 2, SIDE, ROWS, FEAT),
            buf(2, SIDE, ROWS, FEAT),
            buf(SIDE - 1, 2, ROWS, FEAT),
            pltpu.SMEM((SUB, SIDE * SUB), jnp.int32),
            pltpu.SMEM((SUB, SIDE * SUB), jnp.int32),
            pltpu.SemaphoreType.DMA((12,)),
            pltpu.SemaphoreType.DMA((CHUNKS, HALVES, 8)),
            pltpu.SemaphoreType.DMA((CHUNKS, 5)),
            pltpu.SemaphoreType.DMA((2, SIDE)),
            pltpu.SemaphoreType.DMA((4,)),
        ],
        compiler_params=pltpu.CompilerParams(
            collective_id=0, has_side_effects=True, vmem_limit_bytes=48 * 2**20
        ),
    )(
        inputs.reshape(CHUNKS, ROWS, FEAT),
        w_up,
        w_down,
        mask_up,
        mask_down.T,
        cotangent.reshape(CHUNKS, ROWS, FEAT),
    )


def store_kernel(out_here, gin_here, up, down, outputs, grad_inputs, gup, gdown, sems):
    moves = []
    for b in range(SIDE):
        units = pl.ds(b * FEAT, FEAT)
        for k in range(2):
            rows = pl.ds(k * QW, QW)
            there = pl.ds(b * FEAT + k * QW, QW)
            moves.append(pltpu.make_async_copy(up.at[b, rows], gup.at[rows, units], sems.at[4 * b + k]))
            moves.append(pltpu.make_async_copy(down.at[b, rows], gdown.at[there], sems.at[4 * b + 2 + k]))
    moves.append(pltpu.make_async_copy(out_here, outputs, sems.at[4 * SIDE]))
    moves.append(pltpu.make_async_copy(gin_here, grad_inputs, sems.at[4 * SIDE + 1]))
    for copy in moves:
        copy.start()
    for copy in moves:
        copy.wait()


def store(outputs, grad_inputs, up, down):
    vmem = pl.BlockSpec(memory_space=pltpu.VMEM)
    hbm = pl.BlockSpec(memory_space=pl.ANY)
    return pl.pallas_call(
        store_kernel,
        out_shape=[
            jax.ShapeDtypeStruct(outputs.shape, BF16),
            jax.ShapeDtypeStruct(outputs.shape, BF16),
            jax.ShapeDtypeStruct((FEAT, SIDE * FEAT), BF16),
            jax.ShapeDtypeStruct((SIDE * FEAT, FEAT), BF16),
        ],
        in_specs=[vmem] * 4,
        out_specs=[hbm] * 4,
        scratch_shapes=[pltpu.SemaphoreType.DMA((4 * SIDE + 2,))],
        compiler_params=pltpu.CompilerParams(vmem_limit_bytes=8 * 2**20),
    )(outputs, grad_inputs, up, down)


def per_device(inputs, w_up, w_down, mask_up, mask_down, cotangent):
    kept = run_block(inputs, w_up, w_down, mask_up, mask_down, cotangent)
    outputs, grad_inputs, grad_up, grad_down = store(
        *(pltpu.with_memory_space_constraint(array, pltpu.VMEM) for array in kept)
    )
    return (outputs.reshape(inputs.shape), grad_inputs.reshape(inputs.shape), grad_up, grad_down)


def solution(mesh):
    in_specs = (
        P("col", "row"),
        P("row", "col"),
        P("col", "row"),
        P("row", "col"),
        P("col", "row"),
        P("col", "row"),
    )
    out_specs = (P("col", "row"), P("col", "row"), P("row", "col"), P("col", "row"))
    return jax.shard_map(
        per_device, mesh=mesh, in_specs=in_specs, out_specs=out_specs, check_vma=False
    )
```
